128 devices in a mesh: frame: 16 (over x, y), row: 8 (over z, core).
Axes of the slice: x: 4, y: 4, z: 4, core: 2. Of those that a mesh axis runs over, the one named last changes fastest.
Arguments:
- hidden_states: bfloat16 [32, 225, 3072], P('frame', None, 'row'), may hold values from -6 to 6
- timestep_index: int32 [32], P('frame'), may hold values from 0 to 999, as said below
- window_offsets: int32 [32, 2], P('frame'), may hold values from 1 to 4, as said below
- mod_weight: bfloat16 [512, 3, 3072], P('frame', None, 'row'), may hold values from -0.25 to 0.25
- qkv_weight: bfloat16 [3072, 3, 3072], P('frame', None, 'row')
- query_gain: float32 [64], replicated
- key_gain: float32 [64], replicated
- out_weight: bfloat16 [3072, 3072], P('row', 'frame'), may hold values from -0.109375 to 0.109375
- fresh_frame: bfloat16 [225, 3072], P(None, 'row'), may hold values from -6 to 6
Outputs:
- queue_out: bfloat16 [32, 225, 3072], P('frame', None, 'row')
The draws below stay inside these ranges and needn't reach their ends.
Inputs may be any that keep to these rules, and one draw needn't show every extreme that they name: `timestep_index`: levels rise strictly from slot to slot, from 0 at the head slot to 999 at the tail slot. `window_offsets`: some slot has 4 in both columns.
All inputs are finite; a program needn't handle non-finite values.
Results may differ from the reference program's by a relative error of at most 0.009.
Values may be sent and summed in bfloat16 or wider, within the bound.
No kernel may reach another device: no remote copies, remote signals or barrier semaphores. Data moves between devices by JAX's collectives and lax.ppermute only.
A program may use at most 128 MiB of HBM per device.

```python
import math
import jax
import jax.numpy as jnp
from jax import lax

HEADS = 48
HEAD = 64
D = 3072
TEMB = 512
TOKF = 225
REACH = 4
LEVELS = 1000
FRAMES = 32


def draw_timestep_index(key, part):
    key = jax.random.fold_in(key, 11)
    picked = jax.random.permutation(key, LEVELS - 2)[:FRAMES - 2] + 1
    middle = jnp.sort(picked)
    levels = jnp.concatenate([jnp.zeros((1,), jnp.int32), middle.astype(jnp.int32), jnp.full((1,), LEVELS - 1, jnp.int32)])
    return levels.astype(jnp.int32)


def draw_window_offsets(key, part):
    key = jax.random.fold_in(key, 12)
    first, second = jax.random.split(key)
    offsets = jax.random.randint(first, (FRAMES, 2), 1, REACH + 1)
    chosen = jax.random.randint(second, (), 0, FRAMES)
    offsets = offsets.at[chosen].set(REACH)
    return offsets.astype(jnp.int32)


def draw_qkv_weight(key, part):
    key = jax.random.fold_in(key, 13)
    spread = jax.random.normal(key, (D, 3, D), jnp.float32) * D ** (-0.5)
    return spread.astype(jnp.bfloat16)


def gain_draw(key, lower, upper):
    logs = jax.random.uniform(key, (HEAD,), jnp.float32, math.log(lower), math.log(upper))
    return jnp.exp(logs)


def draw_query_gain(key, part):
    key = jax.random.fold_in(key, 14)
    return gain_draw(key, 1.5, 3.0)


def draw_key_gain(key, part):
    key = jax.random.fold_in(key, 15)
    return gain_draw(key, 1.5, 3.0)


def level_of(stream_key, shape, cuts, smallest, largest):
    loudness, own = 1.0, jax.random.fold_in(stream_key, 6)
    for dim, shards_of in cuts:
        steps = jnp.exp(jax.random.uniform(jax.random.fold_in(own, dim), (shards_of,), jnp.float32, smallest / len(cuts), largest / len(cuts)))
        loudness = loudness * jnp.repeat(steps, shape[dim] // shards_of).reshape([-1 if axis == dim else 1 for axis in range(len(shape))])
    return loudness


def gaussian(own_key, extent, width, limit, pieces=(), held_as=jnp.bfloat16):
    values = jax.random.normal(own_key, extent, jnp.float32) * width
    if len(pieces) > 0:
        values = level_of(own_key, extent, pieces, -0.22, 0.18) * values
    return jnp.clip(values, min=-limit, max=limit).astype(held_as)


def setup_inputs(seed: int = 0) -> dict:
    key_of = jax.random.split(jax.random.key(seed), 10)
    hidden_states = gaussian(key_of[0], (FRAMES, TOKF, D), 1.0, 6.0, ((0, 16), (2, 8)))
    timestep_index = draw_timestep_index(jax.random.fold_in(key_of[9], 71), 0)
    window_offsets = draw_window_offsets(jax.random.fold_in(key_of[9], 71), 0)
    mod_weight = gaussian(key_of[3], (TEMB, 3, D), TEMB ** -0.5, 0.25, ((0, 16), (2, 8)))
    qkv_weight = draw_qkv_weight(jax.random.fold_in(key_of[9], 71), 0)
    query_gain = draw_query_gain(jax.random.fold_in(key_of[9], 71), 0)
    key_gain = draw_key_gain(jax.random.fold_in(key_of[9], 71), 0)
    out_weight = gaussian(key_of[7], (D, D), D ** -0.5, 0.109375, ((0, 8), (1, 16)))
    fresh_frame = gaussian(key_of[8], (TOKF, D), 1.0, 6.0, ((1, 8),))
    return {"hidden_states": hidden_states, "timestep_index": timestep_index, "window_offsets": window_offsets, "mod_weight": mod_weight, "qkv_weight": qkv_weight, "query_gain": query_gain, "key_gain": key_gain, "out_weight": out_weight, "fresh_frame": fresh_frame}


def level_embedding(levels):
    half = TEMB // 2
    freqs = jnp.exp(-math.log(10000.0) * jnp.arange(half).astype(jnp.float32) / half)
    angles = levels.astype(jnp.float32)[:, None] * freqs[None, :]
    waves = jnp.concatenate([jnp.cos(angles), jnp.sin(angles)], axis=1)
    return jax.nn.silu(waves).astype(jnp.bfloat16)

def head_norm(values, gain):
    center = lax.optimization_barrier(jnp.mean(values, axis=-1, keepdims=True))
    spread = lax.optimization_barrier(jnp.mean((values - center) ** 2, axis=-1, keepdims=True))
    return ((values - center) * lax.rsqrt(spread + 1e-06) * gain).astype(jnp.bfloat16)

def reference(hidden_states, timestep_index, window_offsets, mod_weight, qkv_weight, query_gain, key_gain, out_weight, fresh_frame):
    embedded = level_embedding(timestep_index)
    modulation = jnp.dot(embedded, mod_weight.reshape(TEMB, 3 * D), preferred_element_type=jnp.float32).reshape(FRAMES, 3, D)
    shift = modulation[:, 0]
    scale = modulation[:, 1]
    gate = modulation[:, 2]
    states = hidden_states.astype(jnp.float32)
    mean = lax.optimization_barrier(jnp.mean(states, axis=2, keepdims=True))
    meansq = lax.optimization_barrier(jnp.mean(states * states, axis=2, keepdims=True))
    normed = (states - mean) * lax.rsqrt(meansq - mean * mean + 1e-05)
    modulated = (normed * (1.0 + scale[:, None, :]) + shift[:, None, :]).astype(jnp.bfloat16)
    projected = jnp.dot(modulated.reshape(FRAMES * TOKF, D), qkv_weight.reshape(D, 3 * D), preferred_element_type=jnp.float32)
    projected = projected.reshape(FRAMES, TOKF, 3, HEADS, HEAD)
    queries = head_norm(projected[:, :, 0], query_gain)
    keys = head_norm(projected[:, :, 1], key_gain)
    values = projected[:, :, 2].astype(jnp.bfloat16)
    queries, keys, values = lax.optimization_barrier((queries, keys, values))
    padding = ((REACH, REACH), (0, 0), (0, 0), (0, 0))
    keys_pad = jnp.pad(keys, padding)
    values_pad = jnp.pad(values, padding)
    span = 2 * REACH + 1
    offsets = jnp.arange(span).astype(jnp.int32) - REACH

    def attend(index):
        query = lax.dynamic_index_in_dim(queries, index, 0, keepdims=False)
        key_win = lax.dynamic_slice_in_dim(keys_pad, index, span, 0).reshape(span * TOKF, HEADS, HEAD)
        value_win = lax.dynamic_slice_in_dim(values_pad, index, span, 0).reshape(span * TOKF, HEADS, HEAD)
        scores = jnp.einsum('qhd,khd->hqk', query.astype(jnp.float32), key_win.astype(jnp.float32)) / math.sqrt(HEAD)
        other = index + offsets
        back = window_offsets[index, 0]
        ahead = window_offsets[index, 1]
        seen = (other >= 0) & (other < FRAMES) & (offsets >= -back) & (offsets <= ahead)
        seen = jnp.repeat(seen, TOKF)
        scores = jnp.where(seen[None, None, :], scores, -jnp.inf)
        top = lax.optimization_barrier(jnp.max(scores, axis=2, keepdims=True))
        expo = jnp.exp(scores - top)
        total = lax.optimization_barrier(jnp.sum(expo, axis=2, keepdims=True))
        weights = lax.optimization_barrier(expo.astype(jnp.bfloat16))
        mixed = jnp.einsum('hqk,khd->qhd', weights.astype(jnp.float32), value_win.astype(jnp.float32))
        mixed = mixed / jnp.transpose(total, (1, 0, 2))
        return mixed.astype(jnp.bfloat16).reshape(TOKF, D)
    mixed_all = lax.map(attend, jnp.arange(FRAMES).astype(jnp.int32))
    attended = jnp.dot(mixed_all.reshape(FRAMES * TOKF, D), out_weight, preferred_element_type=jnp.float32).reshape(FRAMES, TOKF, D)
    updated = (states + gate[:, None, :] * attended).astype(jnp.bfloat16)
    return jnp.concatenate([updated[1:], fresh_frame[None]], axis=0)
```

```python
import math

import jax
import jax.numpy as jnp
from jax import lax
from jax.experimental import pallas as pl
from jax.experimental.pallas import tpu as pltpu
from jax.sharding import PartitionSpec as P

HEAD = 64
D = 3072
TEMB = 512
REACH = 4
SIDE = 4
PADDED = 240
KEYS = 256
PAIR = 2 * HEAD
ORIGIN = (0, -1, 1, 2)


def frame_step(array, over_x, over_y):
    pairs = [
        (x * SIDE + y, (x + over_x) % SIDE * SIDE + (y + over_y) % SIDE)
        for x in range(SIDE)
        for y in range(SIDE)
    ]
    return lax.ppermute(array, "frame", pairs)


def along_x(array, by):
    return frame_step(array, by, 0)


def along_y(array, by):
    return frame_step(array, 0, by)


def along_z(array, by):
    pairs = [(z * 2 + c, (z + by) % SIDE * 2 + c) for z in range(SIDE) for c in range(2)]
    return lax.ppermute(array, "row", pairs)


def other_core(array):
    pairs = [(z * 2 + c, z * 2 + 1 - c) for z in range(SIDE) for c in range(2)]
    return lax.ppermute(array, "row", pairs)


def next_frame(array, by):
    peers = lax.axis_size("frame")
    return lax.ppermute(array, "frame", [(i, (i + by) % peers) for i in range(peers)])


def ring_direct(array, step):
    return [array, step(array, 1), step(array, -1), step(array, 2)]


def ring_relay(array, step):
    below = step(array, 1)
    above = step(array, -1)
    half = array.shape[0] // 2
    return [array, below, above, step(below[:half], 1), step(above[half:], -1)]


def level_embedding(levels):
    half = TEMB // 2
    freqs = jnp.exp(-math.log(10000.0) * jnp.arange(half).astype(jnp.float32) / half)
    angles = levels.astype(jnp.float32)[:, None] * freqs[None, :]
    waves = jnp.concatenate([jnp.cos(angles), jnp.sin(angles)], axis=1)
    return jax.nn.silu(waves).astype(jnp.bfloat16)


def wrap(value, by):
    return lax.rem(value + (by + SIDE), SIDE)


def piece_views(refs):
    views = []
    for hop in range(3):
        views.append([(refs[hop], i) for i in range(SIDE)])
    if len(refs) == SIDE:
        views.append([(refs[3], i) for i in range(SIDE)])
    else:
        views.append([(refs[3], 0), (refs[3], 1), (refs[4], 0), (refs[4], 1)])
    return views


def load_pieces(refs, pos_ref, y_first, rows, source, target, sems, first_sem):
    copies = []
    x = pos_ref[0]
    y = pos_ref[1]
    for outer, line in enumerate(piece_views(refs)):
        for inner, (ref, index) in enumerate(line):
            if y_first:
                over_x, over_y = ORIGIN[outer], ORIGIN[inner]
            else:
                over_x, over_y = ORIGIN[inner], ORIGIN[outer]
            owner = wrap(x, over_x) * SIDE + wrap(y, over_y)
            start = pl.multiple_of(owner * rows, rows)
            copy = pltpu.make_async_copy(
                ref.at[index, source],
                target.at[pl.ds(start, rows)],
                sems.at[first_sem + len(copies)],
            )
            copy.start()
            copies.append(copy)
    return copies


def head_norm_pair(values, gain):
    lane = lax.broadcasted_iota(jnp.int32, values.shape, 1)
    low = lane < HEAD

    def mean_of(array):
        first = jnp.sum(jnp.where(low, array, 0.0), axis=1, keepdims=True)
        second = jnp.sum(jnp.where(low, 0.0, array), axis=1, keepdims=True)
        return jnp.where(low, first, second) * (1.0 / HEAD)

    centered = values - mean_of(values)
    spread = mean_of(centered * centered)
    return (centered * lax.rsqrt(spread + 1e-06) * gain).astype(jnp.bfloat16)


def modulation_kernel(pos_ref, emb_ref, *refs):
    pieces, (out_ref, weight, sems) = refs[:-3], refs[-3:]
    copies = load_pieces(pieces, pos_ref, True, 32, slice(None), weight, sems, 0)
    for copy in copies:
        copy.wait()
    both = jnp.dot(emb_ref[...], weight[...], preferred_element_type=jnp.float32)
    out_ref[0:2] = both[:, :384]
    out_ref[2:4] = both[:, 384:]


def modulate_kernel(pos_ref, own_ref, other_ref, own_mod, other_mod, out_ref):
    tokens = own_ref.shape[2]
    width = own_ref.shape[3]
    z = pos_ref[2]
    core = pos_ref[3]
    for slot in range(2):
        total = jnp.zeros((tokens, width), jnp.float32)
        square = jnp.zeros((tokens, width), jnp.float32)
        for ref in (own_ref, other_ref):
            for hop in range(SIDE):
                part = ref[hop, slot].astype(jnp.float32)
                total += part
                square += part * part
        mean = jnp.sum(total, axis=1, keepdims=True) * (1.0 / D)
        meansq = jnp.sum(square, axis=1, keepdims=True) * (1.0 / D)
        inverse = lax.rsqrt(meansq - mean * mean + 1e-05)
        for ref, mod, at_core in ((own_ref, own_mod, core), (other_ref, other_mod, 1 - core)):
            for hop in range(SIDE):
                part = ref[hop, slot].astype(jnp.float32)
                normed = (part - mean) * inverse
                shift = mod[hop, slot][None]
                scale = mod[hop, 2 + slot][None]
                owner = wrap(z, ORIGIN[hop]) * 2 + at_core
                columns = pl.ds(pl.multiple_of(owner * width, width), width)
                out_ref[slot, 0:tokens, columns] = (normed * (1.0 + scale) + shift).astype(jnp.bfloat16)
        out_ref[slot, tokens:, :] = jnp.zeros((PADDED - tokens, D), jnp.bfloat16)


def key_value_kernel(tokens, count, pos_ref, x_ref, gain_ref, *refs):
    key_refs = refs[:count]
    value_refs = refs[count:-3]
    out_ref, weight, sems = refs[-3:]
    copies = load_pieces(key_refs, pos_ref, True, 192, slice(None), weight.at[:, 0:384], sems, 0)
    copies += load_pieces(value_refs, pos_ref, False, 192, slice(None), weight.at[:, 384:768], sems, 16)
    for copy in copies:
        copy.wait()
    x = x_ref[...].reshape(2 * PADDED, D)
    for block in range(3):
        both = jnp.dot(
            x, weight[:, block * 2 * PAIR : (block + 1) * 2 * PAIR], preferred_element_type=jnp.float32
        )
        for side in range(2):
            group = 2 * block + side
            part = both[:, side * PAIR : (side + 1) * PAIR]
            columns = slice(group % 3 * PAIR, (group % 3 + 1) * PAIR)
            if group < 3:
                part = head_norm_pair(part, gain_ref[...])
                for slot in range(2):
                    rows = part[slot * PADDED : (slot + 1) * PADDED]
                    out_ref[slot, :, columns] = rows
                    out_ref[slot, tokens:, columns] = jnp.broadcast_to(rows[0:1], (PADDED - tokens, PAIR))
            else:
                part = part.astype(jnp.bfloat16)
                for slot in range(2):
                    out_ref[2 + slot, :, columns] = part[slot * PADDED : (slot + 1) * PADDED]


def query_kernel(pos_ref, x_ref, gain_ref, *refs):
    pieces, (out_ref, weight, sems) = refs[:-3], refs[-3:]
    copies = load_pieces(pieces, pos_ref, True, 192, slice(None), weight, sems, 0)
    for copy in copies:
        copy.wait()
    x = x_ref[...].reshape(2 * PADDED, D)
    whole = jnp.dot(x, weight[...], preferred_element_type=jnp.float32)
    for pair in range(3):
        part = head_norm_pair(whole[:, pair * PAIR : (pair + 1) * PAIR], gain_ref[...])
        part = part * jnp.asarray(1.0 / math.sqrt(HEAD), jnp.bfloat16)
        for slot in range(2):
            out_ref[slot, :, pair * PAIR : (pair + 1) * PAIR] = part[slot * PADDED : (slot + 1) * PADDED]


def attention_kernel(tokens, seen_ref, q_ref, m2, m1, own, p1, p2, out_ref, keys, values, scores, top, mix):
    @pl.when(pl.program_id(0) == 0)
    def _():
        row = lax.broadcasted_iota(jnp.int32, (KEYS, PAIR), 0)
        ones = jnp.where(row < tokens, 1.0, 0.0).astype(jnp.bfloat16)
        for slot in range(10):
            values[slot, :, PAIR:] = ones
            values[slot, PADDED:, 0:PAIR] = jnp.zeros((KEYS - PADDED, PAIR), jnp.bfloat16)

    for index, ref in enumerate((m2, m1, own, p1, p2)):
        for half in range(2):
            slot = 2 * index + half
            keys[slot, 0:PADDED, :] = ref[half]
            keys[slot, PADDED:, :] = ref[half, 0 : KEYS - PADDED, :]
            values[slot, 0:PADDED, 0:PAIR] = ref[2 + half]
    lane = lax.broadcasted_iota(jnp.int32, (PADDED, PAIR), 1)
    low = lane < HEAD
    for slot in range(2):
        query = q_ref[slot]
        nothing = jnp.zeros_like(query)
        both = jnp.concatenate([jnp.where(low, query, nothing), jnp.where(low, nothing, query)], axis=0)
        first = seen_ref[2 * slot]
        last = seen_ref[2 * slot + 1]
        top[...] = jnp.full(top.shape, -jnp.inf, jnp.float32)
        mix[...] = jnp.zeros(mix.shape, jnp.float32)

        def score(at, _):
            part = lax.dot_general(
                both, keys[at], (((1,), (1,)), ((), ())), preferred_element_type=jnp.float32
            )
            scores[at] = part
            top[...] = jnp.maximum(top[...], jnp.maximum(part[:, :PAIR], part[:, PAIR:]))
            return 0

        lax.fori_loop(first, last + 1, score, 0)
        peak = jnp.max(top[...], axis=1, keepdims=True)

        def blend(at, _):
            expo = jnp.exp(scores[at] - peak).astype(jnp.bfloat16)
            mix[...] += jnp.dot(expo, values[at], preferred_element_type=jnp.float32)
            return 0

        lax.fori_loop(first, last + 1, blend, 0)
        shares = mix[:, :PAIR] / mix[:, PAIR:]
        out_ref[slot] = jnp.where(low, shares[:PADDED], shares[PADDED:]).astype(jnp.bfloat16)


def out_kernel(tokens, pos_ref, x_ref, *refs):
    pieces, (keep_ref, send_ref, weight, sems) = refs[:-4], refs[-4:]
    copies = load_pieces(pieces, pos_ref, True, 192, slice(0, 192), weight, sems, 0)
    for copy in copies:
        copy.wait()
    x = x_ref[...].reshape(2 * PADDED, 384)
    z = pos_ref[2]
    core = pos_ref[3]
    for ref, at_core in ((send_ref, 1 - core), (keep_ref, core)):
        for hop in range(SIDE):
            owner = lax.rem(z + hop, SIDE) * 2 + at_core
            rows = pl.ds(pl.multiple_of(owner * 384, 384), 384)
            part = lax.dot_general(
                x, weight[rows, :], (((1,), (1,)), ((), ())), preferred_element_type=jnp.float32
            ).astype(jnp.bfloat16)
            for slot in range(2):
                ref[hop, slot] = part[slot * PADDED : slot * PADDED + tokens]


def gate_kernel(pos_ref, emb_ref, *refs):
    pieces, (out_ref, weight, sems) = refs[:-3], refs[-3:]
    copies = load_pieces(pieces, pos_ref, True, 32, slice(192, 224), weight, sems, 0)
    for copy in copies:
        copy.wait()
    out_ref[...] = jnp.dot(emb_ref[...], weight[...], preferred_element_type=jnp.float32)


SMEM = pl.BlockSpec(memory_space=pltpu.SMEM)
VMEM = pl.BlockSpec(memory_space=pltpu.VMEM)
ANY = pl.BlockSpec(memory_space=pl.ANY)


def call(kernel, out_shape, in_specs, scratch, name, flops, moved):
    out_specs = [VMEM] * len(out_shape) if isinstance(out_shape, list) else VMEM
    return pl.pallas_call(
        kernel,
        out_shape=out_shape,
        in_specs=in_specs,
        out_specs=out_specs,
        scratch_shapes=scratch,
        name=name,
        compiler_params=pltpu.CompilerParams(vmem_limit_bytes=48 << 20),
        cost_estimate=pl.CostEstimate(flops=flops, bytes_accessed=moved, transcendentals=0),
    )


def struct(shape, dtype=jnp.bfloat16):
    return jax.ShapeDtypeStruct(shape, dtype)


def per_device(
    hidden_states,
    timestep_index,
    window_offsets,
    mod_weight,
    qkv_weight,
    query_gain,
    key_gain,
    out_weight,
    fresh_frame,
):
    tokens = hidden_states.shape[1]
    width = hidden_states.shape[2]
    place = lax.axis_index("frame")
    row = lax.axis_index("row")
    slots = 2 * lax.axis_size("frame")
    pos = jnp.stack([place // SIDE, place % SIDE, row // 2, row % 2]).astype(jnp.int32)

    head = next_frame(hidden_states[0], -1)
    plan = jnp.concatenate([timestep_index[0:1], window_offsets[0]])
    next_plan = next_frame(plan, -1)
    states = jnp.stack([hidden_states[1], head])
    levels = jnp.stack([timestep_index[1], next_plan[0]])
    back = jnp.stack([window_offsets[1, 0], next_plan[1]])
    ahead = jnp.stack([window_offsets[1, 1], next_plan[2]])

    mod_line = jnp.stack(ring_direct(mod_weight[:, :2].reshape(32, 2 * width), along_y))
    mod_pieces = ring_direct(mod_line, along_x)

    own_states = jnp.stack(ring_direct(states, along_z))
    other_states = other_core(own_states)

    key_line = jnp.stack(ring_direct(qkv_weight[:, 1], along_y))
    value_line = jnp.stack(ring_direct(qkv_weight[:, 2], along_x))
    key_pieces = ring_relay(key_line, along_x)
    value_pieces = ring_relay(value_line, along_y)

    embedded = level_embedding(levels)
    mods = call(
        modulation_kernel,
        struct((4, width), jnp.float32),
        [SMEM, VMEM] + [ANY] * len(mod_pieces),
        [pltpu.VMEM((TEMB, 2 * width), jnp.bfloat16), pltpu.SemaphoreType.DMA((16,))],
        "modulation",
        4 * TEMB * width * 2,
        TEMB * width * 4,
    )(pos, embedded, *mod_pieces)
    own_mods = jnp.stack(ring_direct(mods, along_z))
    other_mods = other_core(own_mods)
    modulated = call(
        modulate_kernel,
        struct((2, PADDED, D)),
        [SMEM] + [VMEM] * 4,
        [],
        "modulate",
        20 * 2 * PADDED * D,
        8 * PADDED * D,
    )(pos, own_states, other_states, own_mods, other_mods)

    key_gains = jnp.tile(key_gain, 2)[None]
    query_gains = jnp.tile(query_gain, 2)[None]
    kv = call(
        lambda *refs: key_value_kernel(tokens, len(key_pieces), *refs),
        struct((4, PADDED, width)),
        [SMEM, VMEM, VMEM] + [ANY] * (len(key_pieces) + len(value_pieces)),
        [pltpu.VMEM((D, 2 * width), jnp.bfloat16), pltpu.SemaphoreType.DMA((32,))],
        "keys_values",
        4 * PADDED * D * 2 * width,
        D * width * 4 + PADDED * D * 4,
    )(pos, modulated, key_gains, *key_pieces, *value_pieces)

    from_m1 = next_frame(kv, 1)
    from_p1 = next_frame(kv, -1)
    from_m2 = next_frame(from_m1, 1)
    from_p2 = next_frame(from_p1, -1)

    query_line = jnp.stack(ring_direct(qkv_weight[:, 0], along_y))
    query_pieces = ring_relay(query_line, along_x)
    out_line = jnp.stack(
        ring_direct(jnp.concatenate([out_weight.T, mod_weight[:, 2]], axis=0), along_y)
    )
    out_pieces = ring_relay(out_line, along_x)

    queries = call(
        query_kernel,
        struct((2, PADDED, width)),
        [SMEM, VMEM, VMEM] + [ANY] * len(query_pieces),
        [pltpu.VMEM((D, width), jnp.bfloat16), pltpu.SemaphoreType.DMA((16,))],
        "queries",
        4 * PADDED * D * width,
        D * width * 2 + PADDED * D * 4,
    )(pos, modulated, query_gains, *query_pieces)

    first_slot = 2 * place + 1
    here = jnp.arange(2, dtype=jnp.int32)
    low = jnp.maximum(here - back, -first_slot) + REACH
    high = jnp.minimum(here + ahead, slots - 1 - first_slot) + REACH
    seen = jnp.stack([low, high], axis=1).reshape(4).astype(jnp.int32)
    kv_block = pl.BlockSpec((4, PADDED, PAIR), lambda pair: (0, 0, pair))
    q_block = pl.BlockSpec((2, PADDED, PAIR), lambda pair: (0, 0, pair))
    mixed = pl.pallas_call(
        lambda *refs: attention_kernel(tokens, *refs),
        out_shape=struct((2, PADDED, width)),
        grid=(3,),
        in_specs=[SMEM, q_block] + [kv_block] * 5,
        out_specs=q_block,
        scratch_shapes=[
            pltpu.VMEM((10, KEYS, PAIR), jnp.bfloat16),
            pltpu.VMEM((10, KEYS, 2 * PAIR), jnp.bfloat16),
            pltpu.VMEM((10, 2 * PADDED, KEYS), jnp.float32),
            pltpu.VMEM((2 * PADDED, PAIR), jnp.float32),
            pltpu.VMEM((2 * PADDED, 2 * PAIR), jnp.float32),
        ],
        name="attention",
        compiler_params=pltpu.CompilerParams(vmem_limit_bytes=48 << 20),
        cost_estimate=pl.CostEstimate(
            flops=6 * 9 * 4 * 480 * 256 * 256, bytes_accessed=6 << 20, transcendentals=54 * 480 * 256
        ),
    )(seen, queries, from_m2, from_m1, kv, from_p1, from_p2)

    keep, send = call(
        lambda *refs: out_kernel(tokens, *refs),
        [struct((SIDE, 2, tokens, width))] * 2,
        [SMEM, VMEM] + [ANY] * len(out_pieces),
        [pltpu.VMEM((D, width), jnp.bfloat16), pltpu.SemaphoreType.DMA((16,))],
        "out_projection",
        4 * PADDED * D * width,
        D * width * 2 + PADDED * D * 4,
    )(pos, mixed, *out_pieces)
    gate = call(
        gate_kernel,
        struct((2, width), jnp.float32),
        [SMEM, VMEM] + [ANY] * len(out_pieces),
        [pltpu.VMEM((TEMB, width), jnp.bfloat16), pltpu.SemaphoreType.DMA((16,))],
        "gate",
        4 * TEMB * width,
        TEMB * width * 4,
    )(pos, embedded, *out_pieces)

    swapped = other_core(send)
    chip = [keep[hop].astype(jnp.float32) + swapped[hop].astype(jnp.float32) for hop in range(SIDE)]
    arrived = [along_z(chip[hop].astype(jnp.bfloat16), hop) for hop in range(1, SIDE)]
    attended = chip[0]
    for part in arrived:
        attended = attended + part.astype(jnp.float32)
    updated = (states.astype(jnp.float32) + gate[:, None, :] * attended).astype(jnp.bfloat16)
    tail = jnp.where(place == lax.axis_size("frame") - 1, fresh_frame, updated[1])
    return jnp.stack([updated[0], tail])


def solution(mesh):
    return jax.shard_map(
        per_device,
        mesh=mesh,
        in_specs=(
            P("frame", None, "row"),
            P("frame"),
            P("frame", None),
            P("frame", None, "row"),
            P("frame", None, "row"),
            P(),
            P(),
            P("row", "frame"),
            P(None, "row"),
        ),
        out_specs=P("frame", None, "row"),
        check_vma=False,
    )
```

```python
import math

import jax
import jax.numpy as jnp
from jax import lax
from jax.experimental import pallas as pl
from jax.experimental.pallas import tpu as pltpu
from jax.sharding import PartitionSpec as P

HEAD = 64
D = 3072
TEMB = 512
REACH = 4
SIDE = 4
PADDED = 240
KEYS = 256
PAIR = 2 * HEAD
ORIGIN = (0, -1, 1, 2)


def torus_step(array, move):
    pairs = []
    for x in range(SIDE):
        for y in range(SIDE):
            for z in range(SIDE):
                for core in range(2):
                    to_x, to_y, to_z = (part % SIDE for part in move(x, y, z, core))
                    pairs.append((device_at(x, y, z, core), device_at(to_x, to_y, to_z, core)))
    return lax.ppermute(array, ("frame", "row"), pairs)


def device_at(x, y, z, core):
    return (x * SIDE + y) * 2 * SIDE + z * 2 + core


def first_step(array, by):
    return torus_step(array, lambda x, y, z, core: (x + by * core, y + by * (1 - core), z))


def second_step(array, by):
    return torus_step(array, lambda x, y, z, core: (x + by * (1 - core), y + by * core, z))


def z_step(array, by):
    return torus_step(array, lambda x, y, z, core: (x, y, z + by * (1 - 2 * core)))


def other_core(array):
    pairs = [(z * 2 + c, z * 2 + 1 - c) for z in range(SIDE) for c in range(2)]
    return lax.ppermute(array, "row", pairs)


def next_frame(array, by):
    peers = lax.axis_size("frame")
    return lax.ppermute(array, "frame", [(i, (i + by) % peers) for i in range(peers)])


def together(*values):
    return lax.optimization_barrier(values)


def level_waves(levels, place):
    half = TEMB // 2
    rows = TEMB // lax.axis_size("frame")
    entry = place * rows + jnp.arange(rows)
    freqs = jnp.exp(-math.log(10000.0) * (entry % half).astype(jnp.float32) / half)
    angles = levels.astype(jnp.float32)[:, None] * freqs[None, :]
    waves = jnp.where(entry[None, :] < half, jnp.cos(angles), jnp.sin(angles))
    return jax.nn.silu(waves).astype(jnp.bfloat16)


def spread(array, axis):
    copies = jnp.broadcast_to(array[None], (lax.axis_size(axis),) + array.shape)
    return lax.all_to_all(copies, axis, 0, 0, tiled=True)


def wrap(value, by):
    return lax.rem(value + by + SIDE, SIDE)


def shard_copies(places, inner_at, outer_at, inner_stride, outer_stride, target, sems):
    copies = []
    for outer in range(SIDE):
        for inner in range(SIDE):
            owner = wrap(outer_at, ORIGIN[outer]) * outer_stride + wrap(inner_at, ORIGIN[inner]) * inner_stride
            copies.append(
                pltpu.make_async_copy(places[outer][inner], target.at[owner], sems.at[len(copies)])
            )
    return copies


def head_norm_pair(values, gain_ref):
    low = lax.broadcasted_iota(jnp.int32, values.shape, 1) < HEAD

    def mean_of(array):
        first = jnp.sum(jnp.where(low, array, 0.0), axis=1, keepdims=True)
        second = jnp.sum(jnp.where(low, 0.0, array), axis=1, keepdims=True)
        return jnp.where(low, first, second) * (1.0 / HEAD)

    gain = jnp.concatenate([gain_ref[...], gain_ref[...]], axis=1)
    centered = values - mean_of(values)
    spread = mean_of(centered * centered)
    return (centered * lax.rsqrt(spread + 1e-06) * gain).astype(jnp.bfloat16)


def modulate(pos_ref, mod_ref, own_refs, other_refs, out_ref):
    tokens = own_refs[0].shape[1]
    width = own_refs[0].shape[2]
    z = pos_ref[4]
    core = pos_ref[5]
    way = pos_ref[6]
    for slot in range(2):
        total = jnp.zeros((tokens, width), jnp.float32)
        square = jnp.zeros((tokens, width), jnp.float32)
        for ref in (*own_refs, *other_refs):
            part = ref[slot].astype(jnp.float32)
            total += part
            square += part * part
        mean = jnp.sum(total, axis=1, keepdims=True) * (1.0 / D)
        meansq = jnp.sum(square, axis=1, keepdims=True) * (1.0 / D)
        inverse = lax.rsqrt(meansq - mean * mean + 1e-05)
        for refs_of, at_core, along in ((own_refs, core, way), (other_refs, 1 - core, -way)):
            for hop in range(SIDE):
                part = refs_of[hop][slot].astype(jnp.float32)
                normed = (part - mean) * inverse
                owner = wrap(z, ORIGIN[hop] * along) * 2 + at_core
                shift = mod_ref[owner, slot : slot + 1, 0:width]
                scale = mod_ref[owner, slot : slot + 1, width : 2 * width]
                columns = pl.ds(pl.multiple_of(owner * width, width), width)
                out_ref[slot, 0:tokens, columns] = (normed * (1.0 + scale) + shift).astype(jnp.bfloat16)
        out_ref[slot, tokens:, :] = jnp.zeros((PADDED - tokens, D), jnp.bfloat16)


def project_kernel(pos_ref, mod_ref, q_gain_ref, k_gain_ref, *refs):
    states, shards, (q_ref, k_ref, v_ref, modulated, weight, sems) = refs[:8], refs[8:24], refs[24:]
    places = [
        [shards[SIDE * outer + inner].at[pl.ds(0, 576)] for inner in range(SIDE)] for outer in range(SIDE)
    ]
    copies = shard_copies(places, pos_ref[0], pos_ref[1], pos_ref[2], pos_ref[3], weight, sems)
    for copy in copies:
        copy.start()
    modulate(pos_ref, mod_ref, states[:SIDE], states[SIDE:], modulated)
    for copy in copies:
        copy.wait()
    x = modulated[...].reshape(2 * PADDED, D)
    for part, target in enumerate((k_ref, v_ref, q_ref)):
        whole = jnp.dot(
            x,
            weight[:, part * 192 : part * 192 + 192, :].reshape(D, 384),
            preferred_element_type=jnp.float32,
        )
        for pair in range(3):
            columns = slice(pair * PAIR, (pair + 1) * PAIR)
            piece = whole[:, columns]
            if part == 0:
                piece = head_norm_pair(piece, k_gain_ref)
            elif part == 1:
                piece = piece.astype(jnp.bfloat16)
            else:
                piece = head_norm_pair(piece, q_gain_ref) * jnp.asarray(1.0 / math.sqrt(HEAD), jnp.bfloat16)
            for slot in range(2):
                target[slot, :, columns] = piece[slot * PADDED : (slot + 1) * PADDED]


def fill_window(pairs, keys, values):
    for index, (key_ref, value_ref) in enumerate(pairs):
        for half in range(2):
            slot = 2 * index + half
            keys[slot, 0:PADDED, :] = key_ref[half]
            keys[slot, PADDED:, :] = jnp.zeros((KEYS - PADDED, PAIR), jnp.bfloat16)
            values[slot, 0:PADDED, 0:PAIR] = value_ref[half]
            values[slot, PADDED:, 0:PAIR] = jnp.zeros((KEYS - PADDED, PAIR), jnp.bfloat16)
            values[slot, :, PAIR:] = jnp.ones((KEYS, PAIR), jnp.bfloat16)


def seen_bias(plan_ref, pos_ref, slot, window, tokens):
    first = 2 * pos_ref[9] + 1
    at = lax.rem(first + slot, plan_ref.shape[0])
    lowest = jnp.maximum(slot - plan_ref[at, 1], -first)
    highest = jnp.minimum(slot + plan_ref[at, 2], plan_ref.shape[0] - 1 - first)
    column = lax.broadcasted_iota(jnp.int32, (1, KEYS), 1)
    parts = []
    for relative in window:
        known = jnp.logical_and(relative >= lowest, relative <= highest)
        count = jnp.where(known, tokens, 0)
        parts.append(jnp.where(column < count, 0.0, -jnp.inf))
    return jnp.concatenate(parts, axis=1)


def near_kernel(tokens, plan_ref, pos_ref, q_ref, km, vm, ko, vo, kp, vp, mix_ref, total_ref, top_ref, keys, values):
    fill_window(((km, vm), (ko, vo), (kp, vp)), keys, values)
    low = lax.broadcasted_iota(jnp.int32, (PADDED, PAIR), 1) < HEAD
    key_win = keys[...].reshape(6 * KEYS, PAIR)
    value_win = values[...].reshape(6 * KEYS, 2 * PAIR)
    for slot in range(2):
        query = q_ref[slot]
        bias = seen_bias(plan_ref, pos_ref, slot, range(-2, 4), tokens)
        nothing = jnp.zeros_like(query)
        mixes = []
        peaks = []
        for one in (jnp.where(low, query, nothing), jnp.where(low, nothing, query)):
            scores = lax.dot_general(
                one, key_win, (((1,), (1,)), ((), ())), preferred_element_type=jnp.float32
            )
            scores = scores + bias
            peak = jnp.max(scores, axis=1, keepdims=True)
            expo = jnp.exp(scores - peak).astype(jnp.bfloat16)
            mixes.append(jnp.dot(expo, value_win, preferred_element_type=jnp.float32))
            peaks.append(jnp.broadcast_to(peak, (PADDED, PAIR)))
        mix_ref[slot] = jnp.where(low, mixes[0][:, :PAIR], mixes[1][:, :PAIR])
        total_ref[slot] = jnp.where(low, mixes[0][:, PAIR:], mixes[1][:, PAIR:])
        top_ref[slot] = jnp.where(low, peaks[0], peaks[1])


def far_kernel(tokens, plan_ref, pos_ref, q_ref, km, vm, kp, vp, mix_ref, total_ref, top_ref, out_ref, keys, values):
    fill_window(((km, vm), (kp, vp)), keys, values)
    low = lax.broadcasted_iota(jnp.int32, (PADDED, PAIR), 1) < HEAD
    window = (-4, -3, 4, 5)
    for slot in range(2):
        query = q_ref[slot]
        bias = seen_bias(plan_ref, pos_ref, slot, window[slot : slot + 3], tokens)
        nothing = jnp.zeros_like(query)
        key_win = keys[slot : slot + 3].reshape(3 * KEYS, PAIR)
        value_win = values[slot : slot + 3].reshape(3 * KEYS, 2 * PAIR)
        near_top = top_ref[slot]
        mixes = []
        peaks = []
        for head, one in enumerate((jnp.where(low, query, nothing), jnp.where(low, nothing, query))):
            scores = lax.dot_general(
                one, key_win, (((1,), (1,)), ((), ())), preferred_element_type=jnp.float32
            )
            scores = scores + bias
            peak = jnp.maximum(
                jnp.max(scores, axis=1, keepdims=True), near_top[:, head * HEAD : head * HEAD + 1]
            )
            expo = jnp.exp(scores - peak).astype(jnp.bfloat16)
            mixes.append(jnp.dot(expo, value_win, preferred_element_type=jnp.float32))
            peaks.append(jnp.broadcast_to(peak, (PADDED, PAIR)))
        fade = jnp.exp(near_top - jnp.where(low, peaks[0], peaks[1]))
        mix = jnp.where(low, mixes[0][:, :PAIR], mixes[1][:, :PAIR]) + mix_ref[slot] * fade
        total = jnp.where(low, mixes[0][:, PAIR:], mixes[1][:, PAIR:]) + total_ref[slot] * fade
        out_ref[slot] = (mix / total).astype(jnp.bfloat16)


def out_kernel(tokens, pos_ref, x_ref, *refs):
    shards, (keep_ref, send_ref, weight, sems) = refs[:16], refs[16:]
    places = [
        [shards[SIDE * outer + inner].at[pl.ds(576, 192)] for inner in range(SIDE)] for outer in range(SIDE)
    ]
    copies = shard_copies(places, pos_ref[0], pos_ref[1], pos_ref[2], pos_ref[3], weight, sems)
    for copy in copies:
        copy.start()
    for copy in copies:
        copy.wait()
    x = x_ref[...].reshape(2 * PADDED, 384)
    z = pos_ref[4]
    core = pos_ref[5]
    way = pos_ref[6]
    for ref, at_core, along in ((send_ref, 1 - core, -way), (keep_ref, core, way)):
        for hop in range(SIDE):
            owner = wrap(z, hop * along) * 2 + at_core
            rows = weight[pl.ds(owner * 2, 2)].reshape(384, 384)
            part = lax.dot_general(
                x, rows, (((1,), (1,)), ((), ())), preferred_element_type=jnp.float32
            ).astype(jnp.bfloat16)
            for slot in range(2):
                ref[2 * hop + slot] = part[slot * PADDED : slot * PADDED + tokens]


SMEM = pl.BlockSpec(memory_space=pltpu.SMEM)
VMEM = pl.BlockSpec(memory_space=pltpu.VMEM)
ANY = pl.BlockSpec(memory_space=pl.ANY)


def call(kernel, out_shape, in_specs, scratch, name, flops, moved, vmem=48):
    out_specs = [VMEM] * len(out_shape) if isinstance(out_shape, list) else VMEM
    return pl.pallas_call(
        kernel,
        out_shape=out_shape,
        in_specs=in_specs,
        out_specs=out_specs,
        scratch_shapes=scratch,
        name=name,
        compiler_params=pltpu.CompilerParams(vmem_limit_bytes=vmem << 20),
        cost_estimate=pl.CostEstimate(flops=flops, bytes_accessed=moved, transcendentals=0),
    )


def struct(shape, dtype=jnp.bfloat16):
    return jax.ShapeDtypeStruct(shape, dtype)


def per_device(
    hidden_states,
    timestep_index,
    window_offsets,
    mod_weight,
    qkv_weight,
    query_gain,
    key_gain,
    out_weight,
    fresh_frame,
):
    tokens = hidden_states.shape[1]
    width = hidden_states.shape[2]
    place = lax.axis_index("frame")
    row = lax.axis_index("row")
    slots = 2 * lax.axis_size("frame")
    first_slot = 2 * place + 1
    x, y, z, core = place // SIDE, place % SIDE, row // 2, row % 2
    pos = jnp.where(core == 0, jnp.stack([y, x, 1, SIDE]), jnp.stack([x, y, SIDE, 1]))
    pos = jnp.concatenate([pos, jnp.stack([z, core, 1 - 2 * core, x, y, place])]).astype(jnp.int32)

    shard = jnp.concatenate(
        [qkv_weight[:, 1], qkv_weight[:, 2], qkv_weight[:, 0], out_weight.T], axis=0
    )

    plan = jnp.concatenate([timestep_index[:, None], window_offsets], axis=1)
    below = first_step(shard, 1)
    above = first_step(shard, -1)
    head = next_frame(hidden_states[0], -1)
    plan = spread(plan, "frame").reshape(slots, 3)
    shard, plan = together(shard, plan)
    own_b = second_step(shard, 1)
    own_a = second_step(shard, -1)
    waves = level_waves(jnp.roll(plan[:, 0], -1), place)
    sums = jnp.dot(waves, mod_weight.reshape(-1, 3 * width), preferred_element_type=jnp.float32)
    states = jnp.stack([hidden_states[1], head])
    sums = lax.all_to_all(sums.reshape(slots // 2, 2, 3 * width), "frame", 0, 0, tiled=True)
    below, above, states, sums = together(below, above, states, sums)
    far = first_step(below, 1)
    below_b = second_step(below, 1)
    below_a = second_step(below, -1)
    above_b = second_step(above, 1)
    above_a = second_step(above, -1)
    z_b = z_step(states, 1)
    z_a = z_step(states, -1)
    far, z_b, z_a = together(far, z_b, z_a)
    far_b = second_step(far, 1)
    far_a = second_step(far, -1)
    own_f = second_step(own_b, 1)
    z_f = z_step(z_b, 1)
    below_f = second_step(below_b, 1)
    above_f = second_step(above_a, -1)
    far_f = second_step(far_a, -1)
    own_states = [states, z_b, z_a, z_f]
    other_states = [other_core(part) for part in own_states]
    mods = jnp.sum(sums, axis=0)
    all_mods = spread(mods, "row")
    shards = [
        shard, below, above, far,
        own_b, below_b, above_b, far_b,
        own_a, below_a, above_a, far_a,
        own_f, below_f, above_f, far_f,
    ]
    queries, keys, values = call(
        project_kernel,
        [struct((2, PADDED, width))] * 3,
        [SMEM] + [VMEM] * 11 + [ANY] * len(shards),
        [
            pltpu.VMEM((2, PADDED, D), jnp.bfloat16),
            pltpu.VMEM((16, 3 * 192, width), jnp.bfloat16),
            pltpu.SemaphoreType.DMA((16,)),
        ],
        "projections",
        4 * PADDED * D * 3 * width,
        D * width * 6 + PADDED * D * 4,
        vmem=60,
    )(pos, all_mods, query_gain[None], key_gain[None], *own_states, *other_states, *shards)

    near = [next_frame(part, by) for part in (keys, values) for by in (1, -1)]
    far_kv = [next_frame(part, by) for part, by in zip(near, (1, -1, 1, -1))]

    block = pl.BlockSpec((2, PADDED, PAIR), lambda pair: (0, 0, pair))
    params = pltpu.CompilerParams(vmem_limit_bytes=48 << 20)
    mix, total, top = pl.pallas_call(
        lambda *refs: near_kernel(tokens, *refs),
        out_shape=[struct((2, PADDED, width), jnp.float32)] * 3,
        grid=(3,),
        in_specs=[SMEM, SMEM] + [block] * 7,
        out_specs=[block] * 3,
        scratch_shapes=[
            pltpu.VMEM((6, KEYS, PAIR), jnp.bfloat16),
            pltpu.VMEM((6, KEYS, 2 * PAIR), jnp.bfloat16),
        ],
        name="attention_near",
        compiler_params=params,
        cost_estimate=pl.CostEstimate(
            flops=6 * 6 * 4 * 480 * 256 * 256, bytes_accessed=6 << 20, transcendentals=36 * 480 * 256
        ),
    )(plan, pos, queries, near[0], near[2], keys, values, near[1], near[3])
    mixed = pl.pallas_call(
        lambda *refs: far_kernel(tokens, *refs),
        out_shape=struct((2, PADDED, width)),
        grid=(3,),
        in_specs=[SMEM, SMEM] + [block] * 8,
        out_specs=block,
        scratch_shapes=[
            pltpu.VMEM((4, KEYS, PAIR), jnp.bfloat16),
            pltpu.VMEM((4, KEYS, 2 * PAIR), jnp.bfloat16),
        ],
        name="attention_far",
        compiler_params=params,
        cost_estimate=pl.CostEstimate(
            flops=6 * 3 * 4 * 480 * 256 * 256, bytes_accessed=6 << 20, transcendentals=18 * 480 * 256
        ),
    )(plan, pos, queries, far_kv[0], far_kv[2], far_kv[1], far_kv[3], mix, total, top)
    keep, send = call(
        lambda *refs: out_kernel(tokens, *refs),
        [struct((2 * SIDE, tokens, width))] * 2,
        [SMEM, VMEM] + [ANY] * len(shards),
        [pltpu.VMEM((16, 192, width), jnp.bfloat16), pltpu.SemaphoreType.DMA((16,))],
        "out_projection",
        4 * PADDED * D * width,
        D * width * 2 + PADDED * D * 4,
    )(pos, mixed, *shards)

    swapped = other_core(send)
    chip = [
        keep[2 * hop : 2 * hop + 2].astype(jnp.float32) + swapped[2 * hop : 2 * hop + 2].astype(jnp.float32)
        for hop in range(SIDE)
    ]
    onward = z_step(chip[2].astype(jnp.bfloat16), 1)
    back = z_step(chip[3].astype(jnp.bfloat16), -1)
    forth = z_step((chip[1] + onward.astype(jnp.float32)).astype(jnp.bfloat16), 1)
    attended = chip[0] + back.astype(jnp.float32) + forth.astype(jnp.float32)
    gate = mods[:, None, 2 * width :]
    updated = (states.astype(jnp.float32) + gate * attended).astype(jnp.bfloat16)
    spare = (first_slot + jnp.arange(2) == slots)[:, None, None]
    return jnp.where(spare, fresh_frame[None], updated)


def solution(mesh):
    return jax.shard_map(
        per_device,
        mesh=mesh,
        in_specs=(
            P("frame", None, "row"),
            P("frame"),
            P("frame", None),
            P("frame", None, "row"),
            P("frame", None, "row"),
            P(),
            P(),
            P("row", "frame"),
            P(None, "row"),
        ),
        out_specs=P("frame", None, "row"),
        check_vma=False,
    )
```

```python
import math

import jax
import jax.numpy as jnp
from jax import lax
from jax.experimental import pallas as pl
from jax.experimental.pallas import tpu as pltpu
from jax.sharding import PartitionSpec as P

HEAD = 64
D = 3072
TEMB = 512
REACH = 4
SIDE = 4
PADDED = 240
KEYS = 256
PAIR = 2 * HEAD
ORIGIN = (0, -1, 1, 2)


def torus_step(array, move):
    pairs = []
    for x in range(SIDE):
        for y in range(SIDE):
            for z in range(SIDE):
                for core in range(2):
                    to_x, to_y, to_z = (part % SIDE for part in move(x, y, z, core))
                    pairs.append((device_at(x, y, z, core), device_at(to_x, to_y, to_z, core)))
    return lax.ppermute(array, ("frame", "row"), pairs)


def device_at(x, y, z, core):
    return (x * SIDE + y) * 2 * SIDE + z * 2 + core


def first_step(array, by):
    return torus_step(array, lambda x, y, z, core: (x + by * core, y + by * (1 - core), z))


def second_step(array, by):
    return torus_step(array, lambda x, y, z, core: (x + by * (1 - core), y + by * core, z))


def z_step(array, by):
    return torus_step(array, lambda x, y, z, core: (x, y, z + by * (1 - 2 * core)))


def other_core(array):
    pairs = [(z * 2 + c, z * 2 + 1 - c) for z in range(SIDE) for c in range(2)]
    return lax.ppermute(array, "row", pairs)


def next_frame(array, by):
    peers = lax.axis_size("frame")
    return lax.ppermute(array, "frame", [(i, (i + by) % peers) for i in range(peers)])


def together(*values):
    return lax.optimization_barrier(values)


def level_waves(levels, place):
    half = TEMB // 2
    rows = TEMB // lax.axis_size("frame")
    entry = place * rows + jnp.arange(rows)
    freqs = jnp.exp(-math.log(10000.0) * (entry % half).astype(jnp.float32) / half)
    angles = levels.astype(jnp.float32)[:, None] * freqs[None, :]
    waves = jnp.where(entry[None, :] < half, jnp.cos(angles), jnp.sin(angles))
    return jax.nn.silu(waves).astype(jnp.bfloat16)


def spread(array, axis):
    copies = jnp.broadcast_to(array[None], (lax.axis_size(axis),) + array.shape)
    return lax.all_to_all(copies, axis, 0, 0, tiled=True)


def wrap(value, by):
    return lax.rem(value + by + SIDE, SIDE)


def shard_copies(places, pos_ref, target, column, sems):
    copies = []
    for outer in range(SIDE):
        for inner in range(SIDE):
            owner = wrap(pos_ref[1], ORIGIN[outer]) * pos_ref[3] + wrap(pos_ref[0], ORIGIN[inner]) * pos_ref[2]
            rows = pl.ds(pl.multiple_of(owner * 192, 192), 192)
            copies.append(
                pltpu.make_async_copy(
                    places[outer][inner], target.at[rows, column : column + 384], sems.at[len(copies)]
                )
            )
    return copies


def head_norm_pair(values, gain_ref):
    low = lax.broadcasted_iota(jnp.int32, values.shape, 1) < HEAD

    def mean_of(array):
        first = jnp.sum(jnp.where(low, array, 0.0), axis=1, keepdims=True)
        second = jnp.sum(jnp.where(low, 0.0, array), axis=1, keepdims=True)
        return jnp.where(low, first, second) * (1.0 / HEAD)

    gain = jnp.concatenate([gain_ref[...], gain_ref[...]], axis=1)
    centered = values - mean_of(values)
    spread = mean_of(centered * centered)
    return (centered * lax.rsqrt(spread + 1e-06) * gain).astype(jnp.bfloat16)


def modulate(pos_ref, mod_ref, own_refs, other_refs, out_ref):
    tokens = own_refs[0].shape[1]
    width = own_refs[0].shape[2]
    z = pos_ref[4]
    core = pos_ref[5]
    way = pos_ref[6]
    for slot in range(2):
        total = jnp.zeros((tokens, width), jnp.float32)
        square = jnp.zeros((tokens, width), jnp.float32)
        for ref in (*own_refs, *other_refs):
            part = ref[slot].astype(jnp.float32)
            total += part
            square += part * part
        mean = jnp.sum(total, axis=1, keepdims=True) * (1.0 / D)
        meansq = jnp.sum(square, axis=1, keepdims=True) * (1.0 / D)
        inverse = lax.rsqrt(meansq - mean * mean + 1e-05)
        for refs_of, at_core, along in ((own_refs, core, way), (other_refs, 1 - core, -way)):
            for hop in range(SIDE):
                part = refs_of[hop][slot].astype(jnp.float32)
                normed = (part - mean) * inverse
                owner = wrap(z, ORIGIN[hop] * along) * 2 + at_core
                shift = mod_ref[owner, slot : slot + 1, 0:width]
                scale = mod_ref[owner, slot : slot + 1, width : 2 * width]
                columns = pl.ds(pl.multiple_of(owner * width, width), width)
                out_ref[slot, 0:tokens, columns] = (normed * (1.0 + scale) + shift).astype(jnp.bfloat16)
        out_ref[slot, tokens:, :] = jnp.zeros((PADDED - tokens, D), jnp.bfloat16)


def shard_places(shards, top):
    return [[shards[SIDE * outer + inner].at[pl.ds(top, 192)] for inner in range(SIDE)] for outer in range(SIDE)]


def key_value_kernel(pos_ref, mod_ref, gain_ref, *refs):
    given, shards = refs[:8], refs[8:24]
    k_ref, v_ref, x_ref, held, modulated, weight, held_sems, x_sem, sems = refs[24:]
    states = [held.at[part] for part in range(8)]
    arriving = [
        pltpu.make_async_copy(given[part], states[part], held_sems.at[part]) for part in range(8)
    ]
    for copy in arriving:
        copy.start()
    copies = [
        shard_copies(shard_places(shards, part * 192), pos_ref, weight, part * 384, sems.at[part])
        for part in range(2)
    ]
    for copy in sum(copies, []):
        copy.start()
    for copy in arriving:
        copy.wait()
    modulate(pos_ref, mod_ref, states[:SIDE], states[SIDE:], modulated)
    x_copy = pltpu.make_async_copy(modulated, x_ref, x_sem)
    x_copy.start()
    x = modulated[...].reshape(2 * PADDED, D)
    for group in range(6):
        if group in (0, 2):
            for copy in copies[group // 2]:
                copy.wait()
        if group % 2 == 0:
            both = jnp.dot(
                x, weight[:, group * PAIR : (group + 2) * PAIR], preferred_element_type=jnp.float32
            )
        piece = both[:, group % 2 * PAIR : (group % 2 + 1) * PAIR]
        columns = slice(group % 3 * PAIR, (group % 3 + 1) * PAIR)
        piece = head_norm_pair(piece, gain_ref) if group < 3 else piece.astype(jnp.bfloat16)
        for slot in range(2):
            (k_ref, v_ref)[group // 3][slot, :, columns] = piece[slot * PADDED : (slot + 1) * PADDED]
    x_copy.wait()


def query_kernel(pos_ref, x_ref, gain_ref, *refs):
    shards, (q_ref, out_weight_ref, weight, sems) = refs[:16], refs[16:]
    copies = shard_copies(shard_places(shards, 384), pos_ref, weight, 0, sems.at[0])
    copies += shard_copies(shard_places(shards, 576), pos_ref, out_weight_ref, 0, sems.at[1])
    for copy in copies:
        copy.start()
    for copy in copies:
        copy.wait()
    x = x_ref[...].reshape(2 * PADDED, D)
    whole = jnp.dot(x, weight[...], preferred_element_type=jnp.float32)
    for pair in range(3):
        columns = slice(pair * PAIR, (pair + 1) * PAIR)
        piece = head_norm_pair(whole[:, columns], gain_ref) * jnp.asarray(1.0 / math.sqrt(HEAD), jnp.bfloat16)
        for slot in range(2):
            q_ref[slot, :, columns] = piece[slot * PADDED : (slot + 1) * PADDED]


def fill_window(pairs, keys, values):
    for index, (key_ref, value_ref) in enumerate(pairs):
        for half in range(2):
            slot = 2 * index + half
            keys[slot, 0:PADDED, :] = key_ref[half]
            keys[slot, PADDED:, :] = jnp.zeros((KEYS - PADDED, PAIR), jnp.bfloat16)
            values[slot, 0:PADDED, 0:PAIR] = value_ref[half]
            values[slot, PADDED:, 0:PAIR] = jnp.zeros((KEYS - PADDED, PAIR), jnp.bfloat16)
            values[slot, :, PAIR:] = jnp.ones((KEYS, PAIR), jnp.bfloat16)


def seen_bias(plan_ref, pos_ref, slot, window, tokens):
    first = 2 * pos_ref[9] + 1
    at = lax.rem(first + slot, plan_ref.shape[0])
    lowest = jnp.maximum(slot - plan_ref[at, 1], -first)
    highest = jnp.minimum(slot + plan_ref[at, 2], plan_ref.shape[0] - 1 - first)
    column = lax.broadcasted_iota(jnp.int32, (1, KEYS), 1)
    parts = []
    for relative in window:
        known = jnp.logical_and(relative >= lowest, relative <= highest)
        count = jnp.where(known, tokens, 0)
        parts.append(jnp.where(column < count, 0.0, -jnp.inf))
    return jnp.concatenate(parts, axis=1)


def near_kernel(tokens, plan_ref, pos_ref, q_ref, km, vm, ko, vo, kp, vp, mix_ref, total_ref, top_ref, keys, values):
    fill_window(((km, vm), (ko, vo), (kp, vp)), keys, values)
    low = lax.broadcasted_iota(jnp.int32, (PADDED, PAIR), 1) < HEAD
    key_win = keys[...].reshape(6 * KEYS, PAIR)
    value_win = values[...].reshape(6 * KEYS, 2 * PAIR)
    for slot in range(2):
        query = q_ref[slot]
        bias = seen_bias(plan_ref, pos_ref, slot, range(-2, 4), tokens)
        nothing = jnp.zeros_like(query)
        mixes = []
        peaks = []
        for one in (jnp.where(low, query, nothing), jnp.where(low, nothing, query)):
            scores = lax.dot_general(
                one, key_win, (((1,), (1,)), ((), ())), preferred_element_type=jnp.float32
            )
            scores = scores + bias
            peak = jnp.max(scores, axis=1, keepdims=True)
            expo = jnp.exp(scores - peak).astype(jnp.bfloat16)
            mixes.append(jnp.dot(expo, value_win, preferred_element_type=jnp.float32))
            peaks.append(jnp.broadcast_to(peak, (PADDED, PAIR)))
        mix_ref[slot] = jnp.where(low, mixes[0][:, :PAIR], mixes[1][:, :PAIR])
        total_ref[slot] = jnp.where(low, mixes[0][:, PAIR:], mixes[1][:, PAIR:])
        top_ref[slot] = jnp.where(low, peaks[0], peaks[1])


def far_kernel(tokens, plan_ref, pos_ref, q_ref, km, vm, kp, vp, mix_ref, total_ref, top_ref, out_ref, keys, values):
    fill_window(((km, vm), (kp, vp)), keys, values)
    low = lax.broadcasted_iota(jnp.int32, (PADDED, PAIR), 1) < HEAD
    window = (-4, -3, 4, 5)
    for slot in range(2):
        query = q_ref[slot]
        bias = seen_bias(plan_ref, pos_ref, slot, window[slot : slot + 3], tokens)
        nothing = jnp.zeros_like(query)
        key_win = keys[slot : slot + 3].reshape(3 * KEYS, PAIR)
        value_win = values[slot : slot + 3].reshape(3 * KEYS, 2 * PAIR)
        near_top = top_ref[slot]
        mixes = []
        peaks = []
        for head, one in enumerate((jnp.where(low, query, nothing), jnp.where(low, nothing, query))):
            scores = lax.dot_general(
                one, key_win, (((1,), (1,)), ((), ())), preferred_element_type=jnp.float32
            )
            scores = scores + bias
            peak = jnp.maximum(
                jnp.max(scores, axis=1, keepdims=True), near_top[:, head * HEAD : head * HEAD + 1]
            )
            expo = jnp.exp(scores - peak).astype(jnp.bfloat16)
            mixes.append(jnp.dot(expo, value_win, preferred_element_type=jnp.float32))
            peaks.append(jnp.broadcast_to(peak, (PADDED, PAIR)))
        fade = jnp.exp(near_top - jnp.where(low, peaks[0], peaks[1]))
        mix = jnp.where(low, mixes[0][:, :PAIR], mixes[1][:, :PAIR]) + mix_ref[slot] * fade
        total = jnp.where(low, mixes[0][:, PAIR:], mixes[1][:, PAIR:]) + total_ref[slot] * fade
        out_ref[slot] = (mix / total).astype(jnp.bfloat16)


def out_kernel(tokens, pos_ref, x_ref, weight, keep_ref, send_ref):
    x = x_ref[...].reshape(2 * PADDED, 384)
    z = pos_ref[4]
    core = pos_ref[5]
    way = pos_ref[6]
    for ref, at_core, along in ((send_ref, 1 - core, -way), (keep_ref, core, way)):
        for hop in range(SIDE):
            owner = wrap(z, hop * along) * 2 + at_core
            rows = weight[pl.ds(pl.multiple_of(owner * 384, 384), 384), :]
            part = lax.dot_general(
                x, rows, (((1,), (1,)), ((), ())), preferred_element_type=jnp.float32
            ).astype(jnp.bfloat16)
            for slot in range(2):
                ref[2 * hop + slot] = part[slot * PADDED : slot * PADDED + tokens]


SMEM = pl.BlockSpec(memory_space=pltpu.SMEM)
VMEM = pl.BlockSpec(memory_space=pltpu.VMEM)
ANY = pl.BlockSpec(memory_space=pl.ANY)


def call(kernel, out_shape, in_specs, scratch, name, flops, moved, vmem=48):
    out_specs = [VMEM] * len(out_shape) if isinstance(out_shape, list) else VMEM
    return pl.pallas_call(
        kernel,
        out_shape=out_shape,
        in_specs=in_specs,
        out_specs=out_specs,
        scratch_shapes=scratch,
        name=name,
        compiler_params=pltpu.CompilerParams(vmem_limit_bytes=vmem << 20),
        cost_estimate=pl.CostEstimate(flops=flops, bytes_accessed=moved, transcendentals=0),
    )


def struct(shape, dtype=jnp.bfloat16):
    return jax.ShapeDtypeStruct(shape, dtype)


def per_device(
    hidden_states,
    timestep_index,
    window_offsets,
    mod_weight,
    qkv_weight,
    query_gain,
    key_gain,
    out_weight,
    fresh_frame,
):
    tokens = hidden_states.shape[1]
    width = hidden_states.shape[2]
    place = lax.axis_index("frame")
    row = lax.axis_index("row")
    slots = 2 * lax.axis_size("frame")
    first_slot = 2 * place + 1
    x, y, z, core = place // SIDE, place % SIDE, row // 2, row % 2
    pos = jnp.where(core == 0, jnp.stack([y, x, 1, SIDE]), jnp.stack([x, y, SIDE, 1]))
    pos = jnp.concatenate([pos, jnp.stack([z, core, 1 - 2 * core, x, y, place])]).astype(jnp.int32)

    shard = jnp.concatenate(
        [qkv_weight[:, 1], qkv_weight[:, 2], qkv_weight[:, 0], out_weight.T], axis=0
    )

    plan = jnp.concatenate([timestep_index[:, None], window_offsets], axis=1)
    below = first_step(shard, 1)
    above = first_step(shard, -1)
    plan = spread(plan, "frame").reshape(slots, 3)
    shard, plan = together(shard, plan)
    own_b = second_step(shard, 1)
    own_a = second_step(shard, -1)
    waves = level_waves(jnp.roll(plan[:, 0], -1), place)
    sums = jnp.dot(waves, mod_weight.reshape(-1, 3 * width), preferred_element_type=jnp.float32)
    sums, first = together(sums, hidden_states[0])
    head = next_frame(first, -1)
    states = jnp.stack([hidden_states[1], head])
    sums = lax.all_to_all(sums.reshape(slots // 2, 2, 3 * width), "frame", 0, 0, tiled=True)
    below, above, states, sums = together(below, above, states, sums)
    far = first_step(below, 1)
    below_b = second_step(below, 1)
    below_a = second_step(below, -1)
    above_b = second_step(above, 1)
    above_a = second_step(above, -1)
    z_b = z_step(states, 1)
    z_a = z_step(states, -1)
    far, z_b, z_a = together(far, z_b, z_a)
    far_b = second_step(far, 1)
    far_a = second_step(far, -1)
    own_f = second_step(own_b, 1)
    z_f = z_step(z_b, 1)
    below_f = second_step(below_b, 1)
    mods = jnp.sum(sums, axis=0)
    all_mods = spread(mods, "row")
    above_f = second_step(above_a, -1)
    far_f = second_step(far_a, -1)
    own_states = [states, z_b, z_a, z_f]
    other_states = [other_core(part) for part in own_states]
    shards = [
        shard, below, above, far,
        own_b, below_b, above_b, far_b,
        own_a, below_a, above_a, far_a,
        own_f, below_f, above_f, far_f,
    ]
    keys, values, modulated = pl.pallas_call(
        key_value_kernel,
        out_shape=[struct((2, PADDED, width))] * 2 + [struct((2, PADDED, D))],
        in_specs=[SMEM] + [VMEM] * 2 + [ANY] * (8 + len(shards)),
        out_specs=[VMEM, VMEM, ANY],
        scratch_shapes=[
            pltpu.VMEM((8, 2, tokens, width), jnp.bfloat16),
            pltpu.VMEM((2, PADDED, D), jnp.bfloat16),
            pltpu.VMEM((D, 2 * width), jnp.bfloat16),
            pltpu.SemaphoreType.DMA((8,)),
            pltpu.SemaphoreType.DMA,
            pltpu.SemaphoreType.DMA((2, 16)),
        ],
        name="keys_values",
        compiler_params=pltpu.CompilerParams(vmem_limit_bytes=60 << 20),
        cost_estimate=pl.CostEstimate(
            flops=4 * PADDED * D * 2 * width, bytes_accessed=D * width * 4 + PADDED * D * 4, transcendentals=0
        ),
    )(pos, all_mods, key_gain[None], *own_states, *other_states, *shards)
    queries, out_whole = call(
        query_kernel,
        [struct((2, PADDED, width)), struct((D, width))],
        [SMEM, VMEM, VMEM] + [ANY] * len(shards),
        [pltpu.VMEM((D, width), jnp.bfloat16), pltpu.SemaphoreType.DMA((2, 16))],
        "queries",
        4 * PADDED * D * width,
        D * width * 4 + PADDED * D * 4,
        vmem=60,
    )(pos, modulated, query_gain[None], *shards)

    near = [next_frame(part, by) for part in (keys, values) for by in (1, -1)]
    far_kv = [next_frame(part, by) for part, by in zip(near, (1, -1, 1, -1))]

    block = pl.BlockSpec((2, PADDED, PAIR), lambda pair: (0, 0, pair))
    params = pltpu.CompilerParams(vmem_limit_bytes=48 << 20)
    mix, total, top = pl.pallas_call(
        lambda *refs: near_kernel(tokens, *refs),
        out_shape=[struct((2, PADDED, width), jnp.float32)] * 3,
        grid=(3,),
        in_specs=[SMEM, SMEM] + [block] * 7,
        out_specs=[block] * 3,
        scratch_shapes=[
            pltpu.VMEM((6, KEYS, PAIR), jnp.bfloat16),
            pltpu.VMEM((6, KEYS, 2 * PAIR), jnp.bfloat16),
        ],
        name="attention_near",
        compiler_params=params,
        cost_estimate=pl.CostEstimate(
            flops=6 * 6 * 4 * 480 * 256 * 256, bytes_accessed=6 << 20, transcendentals=36 * 480 * 256
        ),
    )(plan, pos, queries, near[0], near[2], keys, values, near[1], near[3])
    mixed = pl.pallas_call(
        lambda *refs: far_kernel(tokens, *refs),
        out_shape=struct((2, PADDED, width)),
        grid=(3,),
        in_specs=[SMEM, SMEM] + [block] * 8,
        out_specs=block,
        scratch_shapes=[
            pltpu.VMEM((4, KEYS, PAIR), jnp.bfloat16),
            pltpu.VMEM((4, KEYS, 2 * PAIR), jnp.bfloat16),
        ],
        name="attention_far",
        compiler_params=params,
        cost_estimate=pl.CostEstimate(
            flops=6 * 3 * 4 * 480 * 256 * 256, bytes_accessed=6 << 20, transcendentals=18 * 480 * 256
        ),
    )(plan, pos, queries, far_kv[0], far_kv[2], far_kv[1], far_kv[3], mix, total, top)
    keep, send = call(
        lambda *refs: out_kernel(tokens, *refs),
        [struct((2 * SIDE, tokens, width))] * 2,
        [SMEM, VMEM, VMEM],
        [],
        "out_projection",
        4 * PADDED * D * width,
        D * width * 2 + PADDED * D * 4,
    )(pos, mixed, out_whole)

    swapped = other_core(send)
    chip = [
        keep[2 * hop : 2 * hop + 2].astype(jnp.float32) + swapped[2 * hop : 2 * hop + 2].astype(jnp.float32)
        for hop in range(SIDE)
    ]
    onward = z_step(chip[2].astype(jnp.bfloat16), 1)
    back = z_step(chip[3].astype(jnp.bfloat16), -1)
    forth = z_step((chip[1] + onward.astype(jnp.float32)).astype(jnp.bfloat16), 1)
    attended = chip[0] + back.astype(jnp.float32) + forth.astype(jnp.float32)
    gate = mods[:, None, 2 * width :]
    updated = (states.astype(jnp.float32) + gate * attended).astype(jnp.bfloat16)
    spare = (first_slot + jnp.arange(2) == slots)[:, None, None]
    return jnp.where(spare, fresh_frame[None], updated)


def solution(mesh):
    return jax.shard_map(
        per_device,
        mesh=mesh,
        in_specs=(
            P("frame", None, "row"),
            P("frame"),
            P("frame", None),
            P("frame", None, "row"),
            P("frame", None, "row"),
            P(),
            P(),
            P("row", "frame"),
            P(None, "row"),
        ),
        out_specs=P("frame", None, "row"),
        check_vma=False,
    )
```

```python
import math

import jax
import jax.numpy as jnp
from jax import lax
from jax.experimental import pallas as pl
from jax.experimental.pallas import tpu as pltpu
from jax.sharding import PartitionSpec as P

HEAD = 64
D = 3072
TEMB = 512
REACH = 4
SIDE = 4
PADDED = 240
KEYS = 256
PAIR = 2 * HEAD
ORIGIN = (0, -1, 1, 2)


def torus_step(array, move):
    pairs = []
    for x in range(SIDE):
        for y in range(SIDE):
            for z in range(SIDE):
                for core in range(2):
                    to_x, to_y, to_z = (part % SIDE for part in move(x, y, z, core))
                    pairs.append((device_at(x, y, z, core), device_at(to_x, to_y, to_z, core)))
    return lax.ppermute(array, ("frame", "row"), pairs)


def device_at(x, y, z, core):
    return (x * SIDE + y) * 2 * SIDE + z * 2 + core


def first_step(array, by):
    return torus_step(array, lambda x, y, z, core: (x + by * core, y + by * (1 - core), z))


def second_step(array, by):
    return torus_step(array, lambda x, y, z, core: (x + by * (1 - core), y + by * core, z))


def z_step(array, by):
    return torus_step(array, lambda x, y, z, core: (x, y, z + by * (1 - 2 * core)))


def other_core(array):
    pairs = [(z * 2 + c, z * 2 + 1 - c) for z in range(SIDE) for c in range(2)]
    return lax.ppermute(array, "row", pairs)


def next_frame(array, by):
    peers = lax.axis_size("frame")
    return lax.ppermute(array, "frame", [(i, (i + by) % peers) for i in range(peers)])


def together(*values):
    return lax.optimization_barrier(values)


def level_waves(levels, place):
    half = TEMB // 2
    rows = TEMB // lax.axis_size("frame")
    entry = place * rows + jnp.arange(rows)
    freqs = jnp.exp(-math.log(10000.0) * (entry % half).astype(jnp.float32) / half)
    angles = levels.astype(jnp.float32)[:, None] * freqs[None, :]
    waves = jnp.where(entry[None, :] < half, jnp.cos(angles), jnp.sin(angles))
    return jax.nn.silu(waves).astype(jnp.bfloat16)


def spread(array, axis):
    copies = jnp.broadcast_to(array[None], (lax.axis_size(axis),) + array.shape)
    return lax.all_to_all(copies, axis, 0, 0, tiled=True)


def wrap(value, by):
    return lax.rem(value + by + SIDE, SIDE)


def shard_copies(places, pos_ref, target, column, sems):
    copies = []
    for outer in range(SIDE):
        for inner in range(SIDE):
            owner = wrap(pos_ref[1], ORIGIN[outer]) * pos_ref[3] + wrap(pos_ref[0], ORIGIN[inner]) * pos_ref[2]
            rows = pl.ds(pl.multiple_of(owner * 192, 192), 192)
            copies.append(
                pltpu.make_async_copy(
                    places[outer][inner], target.at[rows, column : column + 384], sems.at[len(copies)]
                )
            )
    return copies


def head_norm_pair(values, gain_ref):
    low = lax.broadcasted_iota(jnp.int32, values.shape, 1) < HEAD

    def mean_of(array):
        first = jnp.sum(jnp.where(low, array, 0.0), axis=1, keepdims=True)
        second = jnp.sum(jnp.where(low, 0.0, array), axis=1, keepdims=True)
        return jnp.where(low, first, second) * (1.0 / HEAD)

    gain = jnp.concatenate([gain_ref[...], gain_ref[...]], axis=1)
    centered = values - mean_of(values)
    spread = mean_of(centered * centered)
    return (centered * lax.rsqrt(spread + 1e-06) * gain).astype(jnp.bfloat16)


def modulate(tokens, pos_ref, own_refs, other_refs, out_ref):
    width = own_refs[0].shape[2]
    z = pos_ref[4]
    core = pos_ref[5]
    way = pos_ref[6]
    for slot in range(2):
        total = jnp.zeros((tokens, width), jnp.float32)
        square = jnp.zeros((tokens, width), jnp.float32)
        for ref in (*own_refs, *other_refs):
            part = ref[slot, 0:tokens, :].astype(jnp.float32)
            total += part
            square += part * part
        mean = jnp.sum(total, axis=1, keepdims=True) * (1.0 / D)
        meansq = jnp.sum(square, axis=1, keepdims=True) * (1.0 / D)
        inverse = lax.rsqrt(meansq - mean * mean + 1e-05)
        for refs_of, at_core, along in ((own_refs, core, way), (other_refs, 1 - core, -way)):
            for hop in range(SIDE):
                part = refs_of[hop][slot, 0:tokens, :].astype(jnp.float32)
                last = refs_of[hop][slot, tokens // 16 * 16 : PADDED, :].astype(jnp.float32)
                first = tokens % 16
                normed = (part - mean) * inverse
                owner = wrap(z, ORIGIN[hop] * along) * 2 + at_core
                shift = last[first : first + 1] + last[first + 1 : first + 2]
                scale = last[first + 2 : first + 3] + last[first + 3 : first + 4]
                columns = pl.ds(pl.multiple_of(owner * width, width), width)
                out_ref[slot, 0:tokens, columns] = (normed * (1.0 + scale) + shift).astype(jnp.bfloat16)
        out_ref[slot, tokens:, :] = jnp.zeros((PADDED - tokens, D), jnp.bfloat16)


def shard_places(shards, top):
    return [[shards[SIDE * outer + inner].at[pl.ds(top, 192)] for inner in range(SIDE)] for outer in range(SIDE)]


def key_value_kernel(tokens, pos_ref, gain_ref, *refs):
    given, shards = refs[:8], refs[8:24]
    k_ref, v_ref, x_ref, held, modulated, weight, held_sems, x_sem, sems = refs[24:]
    states = [held.at[part] for part in range(8)]
    arriving = [
        pltpu.make_async_copy(given[part], states[part], held_sems.at[part]) for part in range(8)
    ]
    for copy in arriving:
        copy.start()
    copies = [
        shard_copies(shard_places(shards, part * 192), pos_ref, weight, part * 384, sems.at[part])
        for part in range(2)
    ]
    for copy in sum(copies, []):
        copy.start()
    for copy in arriving:
        copy.wait()
    modulate(tokens, pos_ref, states[:SIDE], states[SIDE:], modulated)
    x_copy = pltpu.make_async_copy(modulated, x_ref, x_sem)
    x_copy.start()
    x = modulated[...].reshape(2 * PADDED, D)
    for group in range(6):
        if group in (0, 2):
            for copy in copies[group // 2]:
                copy.wait()
        if group % 2 == 0:
            both = jnp.dot(
                x, weight[:, group * PAIR : (group + 2) * PAIR], preferred_element_type=jnp.float32
            )
        piece = both[:, group % 2 * PAIR : (group % 2 + 1) * PAIR]
        columns = slice(group % 3 * PAIR, (group % 3 + 1) * PAIR)
        piece = head_norm_pair(piece, gain_ref) if group < 3 else piece.astype(jnp.bfloat16)
        for slot in range(2):
            (k_ref, v_ref)[group // 3][slot, :, columns] = piece[slot * PADDED : (slot + 1) * PADDED]
    x_copy.wait()


def query_kernel(pos_ref, x_ref, gain_ref, *refs):
    shards, (q_ref, out_weight_ref, weight, sems) = refs[:16], refs[16:]
    copies = shard_copies(shard_places(shards, 384), pos_ref, weight, 0, sems.at[0])
    copies += shard_copies(shard_places(shards, 576), pos_ref, out_weight_ref, 0, sems.at[1])
    for copy in copies:
        copy.start()
    for copy in copies:
        copy.wait()
    x = x_ref[...].reshape(2 * PADDED, D)
    whole = jnp.dot(x, weight[...], preferred_element_type=jnp.float32)
    for pair in range(3):
        columns = slice(pair * PAIR, (pair + 1) * PAIR)
        piece = head_norm_pair(whole[:, columns], gain_ref) * jnp.asarray(1.0 / math.sqrt(HEAD), jnp.bfloat16)
        for slot in range(2):
            q_ref[slot, :, columns] = piece[slot * PADDED : (slot + 1) * PADDED]


def fill_window(pairs, keys, values):
    for index, (key_ref, value_ref) in enumerate(pairs):
        for half in range(2):
            slot = 2 * index + half
            keys[slot, 0:PADDED, :] = key_ref[half]
            keys[slot, PADDED:, :] = jnp.zeros((KEYS - PADDED, PAIR), jnp.bfloat16)
            values[slot, 0:PADDED, 0:PAIR] = value_ref[half]
            values[slot, PADDED:, 0:PAIR] = jnp.zeros((KEYS - PADDED, PAIR), jnp.bfloat16)
            values[slot, :, PAIR:] = jnp.ones((KEYS, PAIR), jnp.bfloat16)


def seen_bias(plan_ref, pos_ref, slot, window, tokens):
    first = 2 * pos_ref[9] + 1
    at = lax.rem(first + slot, plan_ref.shape[0])
    lowest = jnp.maximum(slot - plan_ref[at, 1], -first)
    highest = jnp.minimum(slot + plan_ref[at, 2], plan_ref.shape[0] - 1 - first)
    column = lax.broadcasted_iota(jnp.int32, (1, KEYS), 1)
    parts = []
    for relative in window:
        known = jnp.logical_and(relative >= lowest, relative <= highest)
        count = jnp.where(known, tokens, 0)
        parts.append(jnp.where(column < count, 0.0, -jnp.inf))
    return jnp.concatenate(parts, axis=1)


def near_kernel(tokens, plan_ref, pos_ref, q_ref, km, vm, ko, vo, kp, vp, mix_ref, total_ref, top_ref, keys, values):
    fill_window(((km, vm), (ko, vo), (kp, vp)), keys, values)
    low = lax.broadcasted_iota(jnp.int32, (PADDED, PAIR), 1) < HEAD
    key_win = keys[...].reshape(6 * KEYS, PAIR)
    value_win = values[...].reshape(6 * KEYS, 2 * PAIR)
    for slot in range(2):
        query = q_ref[slot]
        bias = seen_bias(plan_ref, pos_ref, slot, range(-2, 4), tokens)
        nothing = jnp.zeros_like(query)
        mixes = []
        peaks = []
        for one in (jnp.where(low, query, nothing), jnp.where(low, nothing, query)):
            scores = lax.dot_general(
                one, key_win, (((1,), (1,)), ((), ())), preferred_element_type=jnp.float32
            )
            scores = scores + bias
            peak = jnp.max(scores, axis=1, keepdims=True)
            expo = jnp.exp(scores - peak).astype(jnp.bfloat16)
            mixes.append(jnp.dot(expo, value_win, preferred_element_type=jnp.float32))
            peaks.append(jnp.broadcast_to(peak, (PADDED, PAIR)))
        mix_ref[slot] = jnp.where(low, mixes[0][:, :PAIR], mixes[1][:, :PAIR])
        total_ref[slot] = jnp.where(low, mixes[0][:, PAIR:], mixes[1][:, PAIR:])
        top_ref[slot] = jnp.where(low, peaks[0], peaks[1])


def far_kernel(tokens, plan_ref, pos_ref, q_ref, km, vm, kp, vp, mix_ref, total_ref, top_ref, out_ref, keys, values):
    fill_window(((km, vm), (kp, vp)), keys, values)
    low = lax.broadcasted_iota(jnp.int32, (PADDED, PAIR), 1) < HEAD
    window = (-4, -3, 4, 5)
    for slot in range(2):
        query = q_ref[slot]
        bias = seen_bias(plan_ref, pos_ref, slot, window[slot : slot + 3], tokens)
        nothing = jnp.zeros_like(query)
        key_win = keys[slot : slot + 3].reshape(3 * KEYS, PAIR)
        value_win = values[slot : slot + 3].reshape(3 * KEYS, 2 * PAIR)
        near_top = top_ref[slot]
        mixes = []
        peaks = []
        for head, one in enumerate((jnp.where(low, query, nothing), jnp.where(low, nothing, query))):
            scores = lax.dot_general(
                one, key_win, (((1,), (1,)), ((), ())), preferred_element_type=jnp.float32
            )
            scores = scores + bias
            peak = jnp.maximum(
                jnp.max(scores, axis=1, keepdims=True), near_top[:, head * HEAD : head * HEAD + 1]
            )
            expo = jnp.exp(scores - peak).astype(jnp.bfloat16)
            mixes.append(jnp.dot(expo, value_win, preferred_element_type=jnp.float32))
            peaks.append(jnp.broadcast_to(peak, (PADDED, PAIR)))
        fade = jnp.exp(near_top - jnp.where(low, peaks[0], peaks[1]))
        mix = jnp.where(low, mixes[0][:, :PAIR], mixes[1][:, :PAIR]) + mix_ref[slot] * fade
        total = jnp.where(low, mixes[0][:, PAIR:], mixes[1][:, PAIR:]) + total_ref[slot] * fade
        out_ref[slot] = (mix / total).astype(jnp.bfloat16)


def out_kernel(tokens, pos_ref, x_ref, weight, keep_ref, send_ref):
    x = x_ref[...].reshape(2 * PADDED, 384)
    z = pos_ref[4]
    core = pos_ref[5]
    way = pos_ref[6]
    for ref, at_core, along in ((send_ref, 1 - core, -way), (keep_ref, core, way)):
        for hop in range(SIDE):
            owner = wrap(z, hop * along) * 2 + at_core
            rows = weight[pl.ds(pl.multiple_of(owner * 384, 384), 384), :]
            part = lax.dot_general(
                x, rows, (((1,), (1,)), ((), ())), preferred_element_type=jnp.float32
            ).astype(jnp.bfloat16)
            for slot in range(2):
                ref[2 * hop + slot] = part[slot * PADDED : slot * PADDED + tokens]


SMEM = pl.BlockSpec(memory_space=pltpu.SMEM)
VMEM = pl.BlockSpec(memory_space=pltpu.VMEM)
ANY = pl.BlockSpec(memory_space=pl.ANY)


def call(kernel, out_shape, in_specs, scratch, name, flops, moved, vmem=48):
    out_specs = [VMEM] * len(out_shape) if isinstance(out_shape, list) else VMEM
    return pl.pallas_call(
        kernel,
        out_shape=out_shape,
        in_specs=in_specs,
        out_specs=out_specs,
        scratch_shapes=scratch,
        name=name,
        compiler_params=pltpu.CompilerParams(vmem_limit_bytes=vmem << 20),
        cost_estimate=pl.CostEstimate(flops=flops, bytes_accessed=moved, transcendentals=0),
    )


def struct(shape, dtype=jnp.bfloat16):
    return jax.ShapeDtypeStruct(shape, dtype)


def per_device(
    hidden_states,
    timestep_index,
    window_offsets,
    mod_weight,
    qkv_weight,
    query_gain,
    key_gain,
    out_weight,
    fresh_frame,
):
    tokens = hidden_states.shape[1]
    width = hidden_states.shape[2]
    place = lax.axis_index("frame")
    row = lax.axis_index("row")
    slots = 2 * lax.axis_size("frame")
    first_slot = 2 * place + 1
    x, y, z, core = place // SIDE, place % SIDE, row // 2, row % 2
    pos = jnp.where(core == 0, jnp.stack([y, x, 1, SIDE]), jnp.stack([x, y, SIDE, 1]))
    pos = jnp.concatenate([pos, jnp.stack([z, core, 1 - 2 * core, x, y, place])]).astype(jnp.int32)

    shard = jnp.concatenate(
        [qkv_weight[:, 1], qkv_weight[:, 2], qkv_weight[:, 0], out_weight.T], axis=0
    )

    plan = jnp.concatenate([timestep_index[:, None], window_offsets], axis=1)
    below = first_step(shard, 1)
    above = first_step(shard, -1)
    plan = spread(plan, "frame").reshape(slots, 3)
    shard, plan = together(shard, plan)
    own_b = second_step(shard, 1)
    own_a = second_step(shard, -1)
    waves = level_waves(jnp.roll(plan[:, 0], -1), place)
    sums = jnp.dot(waves, mod_weight.reshape(-1, 3 * width), preferred_element_type=jnp.float32)
    sums, first = together(sums, hidden_states[0])
    head = next_frame(first, -1)
    states = jnp.stack([hidden_states[1], head])
    sums = lax.all_to_all(sums.reshape(slots // 2, 2, 3 * width), "frame", 0, 0, tiled=True)
    travelling = jnp.pad(states, ((0, 0), (0, PADDED - tokens), (0, 0)))
    below, above, travelling, sums = together(below, above, travelling, sums)
    mods = jnp.sum(sums, axis=0)
    near_mods = lax.reduce_precision(mods, 8, 7)
    pieces = [near_mods[:, :width], (mods - near_mods)[:, :width]]
    pieces += [near_mods[:, width : 2 * width], (mods - near_mods)[:, width : 2 * width]]
    pieces = jnp.stack(pieces, axis=1).astype(jnp.bfloat16)
    travelling = lax.dynamic_update_slice(travelling, pieces, (0, tokens, 0))
    far = first_step(below, 1)
    below_b = second_step(below, 1)
    below_a = second_step(below, -1)
    above_b = second_step(above, 1)
    above_a = second_step(above, -1)
    z_b = z_step(travelling, 1)
    z_a = z_step(travelling, -1)
    far, z_b, z_a = together(far, z_b, z_a)
    far_b = second_step(far, 1)
    far_a = second_step(far, -1)
    own_f = second_step(own_b, 1)
    z_f = z_step(z_b, 1)
    below_f = second_step(below_b, 1)
    above_f = second_step(above_a, -1)
    far_f = second_step(far_a, -1)
    own_states = [travelling, z_b, z_a, z_f]
    other_states = [other_core(part) for part in own_states]
    shards = [
        shard, below, above, far,
        own_b, below_b, above_b, far_b,
        own_a, below_a, above_a, far_a,
        own_f, below_f, above_f, far_f,
    ]
    keys, values, modulated = pl.pallas_call(
        lambda *refs: key_value_kernel(tokens, *refs),
        out_shape=[struct((2, PADDED, width))] * 2 + [struct((2, PADDED, D))],
        in_specs=[SMEM, VMEM] + [ANY] * (8 + len(shards)),
        out_specs=[VMEM, VMEM, ANY],
        scratch_shapes=[
            pltpu.VMEM((8, 2, PADDED, width), jnp.bfloat16),
            pltpu.VMEM((2, PADDED, D), jnp.bfloat16),
            pltpu.VMEM((D, 2 * width), jnp.bfloat16),
            pltpu.SemaphoreType.DMA((8,)),
            pltpu.SemaphoreType.DMA,
            pltpu.SemaphoreType.DMA((2, 16)),
        ],
        name="keys_values",
        compiler_params=pltpu.CompilerParams(vmem_limit_bytes=60 << 20),
        cost_estimate=pl.CostEstimate(
            flops=4 * PADDED * D * 2 * width, bytes_accessed=D * width * 4 + PADDED * D * 4, transcendentals=0
        ),
    )(pos, key_gain[None], *own_states, *other_states, *shards)
    queries, out_whole = call(
        query_kernel,
        [struct((2, PADDED, width)), struct((D, width))],
        [SMEM, VMEM, VMEM] + [ANY] * len(shards),
        [pltpu.VMEM((D, width), jnp.bfloat16), pltpu.SemaphoreType.DMA((2, 16))],
        "queries",
        4 * PADDED * D * width,
        D * width * 4 + PADDED * D * 4,
        vmem=60,
    )(pos, modulated, query_gain[None], *shards)

    near = [next_frame(part, by) for part in (keys, values) for by in (1, -1)]
    far_kv = [next_frame(part, by) for part, by in zip(near, (1, -1, 1, -1))]

    block = pl.BlockSpec((2, PADDED, PAIR), lambda pair: (0, 0, pair))
    params = pltpu.CompilerParams(vmem_limit_bytes=48 << 20)
    mix, total, top = pl.pallas_call(
        lambda *refs: near_kernel(tokens, *refs),
        out_shape=[struct((2, PADDED, width), jnp.float32)] * 3,
        grid=(3,),
        in_specs=[SMEM, SMEM] + [block] * 7,
        out_specs=[block] * 3,
        scratch_shapes=[
            pltpu.VMEM((6, KEYS, PAIR), jnp.bfloat16),
            pltpu.VMEM((6, KEYS, 2 * PAIR), jnp.bfloat16),
        ],
        name="attention_near",
        compiler_params=params,
        cost_estimate=pl.CostEstimate(
            flops=6 * 6 * 4 * 480 * 256 * 256, bytes_accessed=6 << 20, transcendentals=36 * 480 * 256
        ),
    )(plan, pos, queries, near[0], near[2], keys, values, near[1], near[3])
    mixed = pl.pallas_call(
        lambda *refs: far_kernel(tokens, *refs),
        out_shape=struct((2, PADDED, width)),
        grid=(3,),
        in_specs=[SMEM, SMEM] + [block] * 8,
        out_specs=block,
        scratch_shapes=[
            pltpu.VMEM((4, KEYS, PAIR), jnp.bfloat16),
            pltpu.VMEM((4, KEYS, 2 * PAIR), jnp.bfloat16),
        ],
        name="attention_far",
        compiler_params=params,
        cost_estimate=pl.CostEstimate(
            flops=6 * 3 * 4 * 480 * 256 * 256, bytes_accessed=6 << 20, transcendentals=18 * 480 * 256
        ),
    )(plan, pos, queries, far_kv[0], far_kv[2], far_kv[1], far_kv[3], mix, total, top)
    keep, send = call(
        lambda *refs: out_kernel(tokens, *refs),
        [struct((2 * SIDE, tokens, width))] * 2,
        [SMEM, VMEM, VMEM],
        [],
        "out_projection",
        4 * PADDED * D * width,
        D * width * 2 + PADDED * D * 4,
    )(pos, mixed, out_whole)

    swapped = other_core(send)
    chip = [
        keep[2 * hop : 2 * hop + 2].astype(jnp.float32) + swapped[2 * hop : 2 * hop + 2].astype(jnp.float32)
        for hop in range(SIDE)
    ]
    onward = z_step(chip[2].astype(jnp.bfloat16), 1)
    back = z_step(chip[3].astype(jnp.bfloat16), -1)
    forth = z_step((chip[1] + onward.astype(jnp.float32)).astype(jnp.bfloat16), 1)
    attended = chip[0] + back.astype(jnp.float32) + forth.astype(jnp.float32)
    gate = mods[:, None, 2 * width :]
    updated = (states.astype(jnp.float32) + gate * attended).astype(jnp.bfloat16)
    spare = (first_slot + jnp.arange(2) == slots)[:, None, None]
    return jnp.where(spare, fresh_frame[None], updated)


def solution(mesh):
    return jax.shard_map(
        per_device,
        mesh=mesh,
        in_specs=(
            P("frame", None, "row"),
            P("frame"),
            P("frame", None),
            P("frame", None, "row"),
            P("frame", None, "row"),
            P(),
            P(),
            P("row", "frame"),
            P(None, "row"),
        ),
        out_specs=P("frame", None, "row"),
        check_vma=False,
    )
```

```python
import math

import jax
import jax.numpy as jnp
from jax import lax
from jax.experimental import pallas as pl
from jax.experimental.pallas import tpu as pltpu
from jax.sharding import PartitionSpec as P

HEAD = 64
D = 3072
TEMB = 512
REACH = 4
SIDE = 4
PADDED = 240
KEYS = 256
PAIR = 2 * HEAD
ORIGIN = (0, -1, 1, 2)


def torus_step(array, move):
    pairs = []
    for x in range(SIDE):
        for y in range(SIDE):
            for z in range(SIDE):
                for core in range(2):
                    to_x, to_y, to_z = (part % SIDE for part in move(x, y, z, core))
                    pairs.append((device_at(x, y, z, core), device_at(to_x, to_y, to_z, core)))
    return lax.ppermute(array, ("frame", "row"), pairs)


def device_at(x, y, z, core):
    return (x * SIDE + y) * 2 * SIDE + z * 2 + core


def first_step(array, by):
    return torus_step(array, lambda x, y, z, core: (x + by * core, y + by * (1 - core), z))


def second_step(array, by):
    return torus_step(array, lambda x, y, z, core: (x + by * (1 - core), y + by * core, z))


def z_step(array, by):
    return torus_step(array, lambda x, y, z, core: (x, y, z + by * (1 - 2 * core)))


def other_core(array):
    pairs = [(z * 2 + c, z * 2 + 1 - c) for z in range(SIDE) for c in range(2)]
    return lax.ppermute(array, "row", pairs)


def next_frame(array, by):
    peers = lax.axis_size("frame")
    return lax.ppermute(array, "frame", [(i, (i + by) % peers) for i in range(peers)])


def together(*values):
    return lax.optimization_barrier(values)


def level_waves(levels, place):
    half = TEMB // 2
    rows = TEMB // lax.axis_size("frame")
    entry = place * rows + jnp.arange(rows)
    freqs = jnp.exp(-math.log(10000.0) * (entry % half).astype(jnp.float32) / half)
    angles = levels.astype(jnp.float32)[:, None] * freqs[None, :]
    waves = jnp.where(entry[None, :] < half, jnp.cos(angles), jnp.sin(angles))
    return jax.nn.silu(waves).astype(jnp.bfloat16)


def spread(array, axis):
    copies = jnp.broadcast_to(array[None], (lax.axis_size(axis),) + array.shape)
    return lax.all_to_all(copies, axis, 0, 0, tiled=True)


def wrap(value, by):
    return lax.rem(value + by + SIDE, SIDE)


def shard_copies(places, pos_ref, target, column, sems):
    copies = []
    for outer in range(SIDE):
        for inner in range(SIDE):
            owner = wrap(pos_ref[1], ORIGIN[outer]) * pos_ref[3] + wrap(pos_ref[0], ORIGIN[inner]) * pos_ref[2]
            rows = pl.ds(pl.multiple_of(owner * 192, 192), 192)
            copies.append(
                pltpu.make_async_copy(
                    places[outer][inner], target.at[rows, column : column + 384], sems.at[len(copies)]
                )
            )
    return copies


def head_norm_pair(values, gain_ref):
    low = lax.broadcasted_iota(jnp.int32, values.shape, 1) < HEAD

    def mean_of(array):
        first = jnp.sum(jnp.where(low, array, 0.0), axis=1, keepdims=True)
        second = jnp.sum(jnp.where(low, 0.0, array), axis=1, keepdims=True)
        return jnp.where(low, first, second) * (1.0 / HEAD)

    gain = jnp.concatenate([gain_ref[...], gain_ref[...]], axis=1)
    centered = values - mean_of(values)
    spread = mean_of(centered * centered)
    return (centered * lax.rsqrt(spread + 1e-06) * gain).astype(jnp.bfloat16)


def modulate(tokens, pos_ref, own_refs, other_refs, out_ref, arriving):
    width = own_refs[0].shape[2]
    z = pos_ref[4]
    core = pos_ref[5]
    way = pos_ref[6]
    for slot in range(2):
        for copy in arriving[slot]:
            copy.wait()
        total = jnp.zeros((tokens, width), jnp.float32)
        square = jnp.zeros((tokens, width), jnp.float32)
        for ref in (*own_refs, *other_refs):
            part = ref[slot, 0:tokens, :].astype(jnp.float32)
            total += part
            square += part * part
        mean = jnp.sum(total, axis=1, keepdims=True) * (1.0 / D)
        meansq = jnp.sum(square, axis=1, keepdims=True) * (1.0 / D)
        inverse = lax.rsqrt(meansq - mean * mean + 1e-05)
        for refs_of, at_core, along in ((own_refs, core, way), (other_refs, 1 - core, -way)):
            for hop in range(SIDE):
                part = refs_of[hop][slot, 0:tokens, :].astype(jnp.float32)
                last = refs_of[hop][slot, tokens // 16 * 16 : PADDED, :].astype(jnp.float32)
                first = tokens % 16
                normed = (part - mean) * inverse
                owner = wrap(z, ORIGIN[hop] * along) * 2 + at_core
                shift = last[first : first + 1] + last[first + 1 : first + 2]
                scale = last[first + 2 : first + 3] + last[first + 3 : first + 4]
                columns = pl.ds(pl.multiple_of(owner * width, width), width)
                out_ref[slot, 0:tokens, columns] = (normed * (1.0 + scale) + shift).astype(jnp.bfloat16)
        out_ref[slot, tokens:, :] = jnp.zeros((PADDED - tokens, D), jnp.bfloat16)


def shard_places(shards, top):
    return [[shards[SIDE * outer + inner].at[pl.ds(top, 192)] for inner in range(SIDE)] for outer in range(SIDE)]


def key_value_kernel(tokens, pos_ref, gain_ref, *refs):
    given, shards = refs[:8], refs[8:24]
    k_ref, v_ref, x_ref, held, modulated, weight, held_sems, x_sem, sems = refs[24:]
    states = [held.at[part] for part in range(8)]
    arriving = [
        [
            pltpu.make_async_copy(given[part].at[slot], states[part].at[slot], held_sems.at[slot, part])
            for part in range(8)
        ]
        for slot in range(2)
    ]
    for copy in sum(arriving, []):
        copy.start()
    copies = [
        shard_copies(shard_places(shards, part * 192), pos_ref, weight, part * 384, sems.at[part])
        for part in range(2)
    ]
    for copy in sum(copies, []):
        copy.start()
    modulate(tokens, pos_ref, states[:SIDE], states[SIDE:], modulated, arriving)
    x_copy = pltpu.make_async_copy(modulated, x_ref, x_sem)
    x_copy.start()
    x = modulated[...].reshape(2 * PADDED, D)
    for group in range(6):
        if group in (0, 2):
            for copy in copies[group // 2]:
                copy.wait()
        if group % 2 == 0:
            both = jnp.dot(
                x, weight[:, group * PAIR : (group + 2) * PAIR], preferred_element_type=jnp.float32
            )
        piece = both[:, group % 2 * PAIR : (group % 2 + 1) * PAIR]
        columns = slice(group % 3 * PAIR, (group % 3 + 1) * PAIR)
        piece = head_norm_pair(piece, gain_ref) if group < 3 else piece.astype(jnp.bfloat16)
        for slot in range(2):
            (k_ref, v_ref)[group // 3][slot, :, columns] = piece[slot * PADDED : (slot + 1) * PADDED]
    x_copy.wait()


def query_kernel(pos_ref, x_ref, gain_ref, *refs):
    shards, (q_ref, out_weight_ref, weight, sems) = refs[:16], refs[16:]
    copies = shard_copies(shard_places(shards, 384), pos_ref, weight, 0, sems.at[0])
    copies += shard_copies(shard_places(shards, 576), pos_ref, out_weight_ref, 0, sems.at[1])
    for copy in copies:
        copy.start()
    for copy in copies:
        copy.wait()
    x = x_ref[...].reshape(2 * PADDED, D)
    whole = jnp.dot(x, weight[...], preferred_element_type=jnp.float32)
    for pair in range(3):
        columns = slice(pair * PAIR, (pair + 1) * PAIR)
        piece = head_norm_pair(whole[:, columns], gain_ref) * jnp.asarray(1.0 / math.sqrt(HEAD), jnp.bfloat16)
        for slot in range(2):
            q_ref[slot, :, columns] = piece[slot * PADDED : (slot + 1) * PADDED]


def fill_window(pairs, keys, values):
    for index, (key_ref, value_ref) in enumerate(pairs):
        for half in range(2):
            slot = 2 * index + half
            keys[slot, 0:PADDED, :] = key_ref[half]
            keys[slot, PADDED:, :] = jnp.zeros((KEYS - PADDED, PAIR), jnp.bfloat16)
            values[slot, 0:PADDED, 0:PAIR] = value_ref[half]
            values[slot, PADDED:, 0:PAIR] = jnp.zeros((KEYS - PADDED, PAIR), jnp.bfloat16)
            values[slot, :, PAIR:] = jnp.ones((KEYS, PAIR), jnp.bfloat16)


def seen_bias(plan_ref, pos_ref, slot, window, tokens):
    first = 2 * pos_ref[9] + 1
    at = lax.rem(first + slot, plan_ref.shape[0])
    lowest = jnp.maximum(slot - plan_ref[at, 1], -first)
    highest = jnp.minimum(slot + plan_ref[at, 2], plan_ref.shape[0] - 1 - first)
    column = lax.broadcasted_iota(jnp.int32, (1, KEYS), 1)
    parts = []
    for relative in window:
        known = jnp.logical_and(relative >= lowest, relative <= highest)
        count = jnp.where(known, tokens, 0)
        parts.append(jnp.where(column < count, 0.0, -jnp.inf))
    return jnp.concatenate(parts, axis=1)


def near_kernel(tokens, plan_ref, pos_ref, q_ref, km, vm, ko, vo, kp, vp, mix_ref, total_ref, top_ref, keys, values):
    fill_window(((km, vm), (ko, vo), (kp, vp)), keys, values)
    low = lax.broadcasted_iota(jnp.int32, (PADDED, PAIR), 1) < HEAD
    key_win = keys[...].reshape(6 * KEYS, PAIR)
    value_win = values[...].reshape(6 * KEYS, 2 * PAIR)
    for slot in range(2):
        query = q_ref[slot]
        bias = seen_bias(plan_ref, pos_ref, slot, range(-2, 4), tokens)
        nothing = jnp.zeros_like(query)
        mixes = []
        peaks = []
        for one in (jnp.where(low, query, nothing), jnp.where(low, nothing, query)):
            scores = lax.dot_general(
                one, key_win, (((1,), (1,)), ((), ())), preferred_element_type=jnp.float32
            )
            scores = scores + bias
            peak = jnp.max(scores, axis=1, keepdims=True)
            expo = jnp.exp(scores - peak).astype(jnp.bfloat16)
            mixes.append(jnp.dot(expo, value_win, preferred_element_type=jnp.float32))
            peaks.append(jnp.broadcast_to(peak, (PADDED, PAIR)))
        mix_ref[slot] = jnp.where(low, mixes[0][:, :PAIR], mixes[1][:, :PAIR])
        total_ref[slot] = jnp.where(low, mixes[0][:, PAIR:], mixes[1][:, PAIR:])
        top_ref[slot] = jnp.where(low, peaks[0], peaks[1])


def far_kernel(tokens, plan_ref, pos_ref, q_ref, km, vm, kp, vp, mix_ref, total_ref, top_ref, out_ref, keys, values):
    fill_window(((km, vm), (kp, vp)), keys, values)
    low = lax.broadcasted_iota(jnp.int32, (PADDED, PAIR), 1) < HEAD
    window = (-4, -3, 4, 5)
    for slot in range(2):
        query = q_ref[slot]
        bias = seen_bias(plan_ref, pos_ref, slot, window[slot : slot + 3], tokens)
        nothing = jnp.zeros_like(query)
        key_win = keys[slot : slot + 3].reshape(3 * KEYS, PAIR)
        value_win = values[slot : slot + 3].reshape(3 * KEYS, 2 * PAIR)
        near_top = top_ref[slot]
        mixes = []
        peaks = []
        for head, one in enumerate((jnp.where(low, query, nothing), jnp.where(low, nothing, query))):
            scores = lax.dot_general(
                one, key_win, (((1,), (1,)), ((), ())), preferred_element_type=jnp.float32
            )
            scores = scores + bias
            peak = jnp.maximum(
                jnp.max(scores, axis=1, keepdims=True), near_top[:, head * HEAD : head * HEAD + 1]
            )
            expo = jnp.exp(scores - peak).astype(jnp.bfloat16)
            mixes.append(jnp.dot(expo, value_win, preferred_element_type=jnp.float32))
            peaks.append(jnp.broadcast_to(peak, (PADDED, PAIR)))
        fade = jnp.exp(near_top - jnp.where(low, peaks[0], peaks[1]))
        mix = jnp.where(low, mixes[0][:, :PAIR], mixes[1][:, :PAIR]) + mix_ref[slot] * fade
        total = jnp.where(low, mixes[0][:, PAIR:], mixes[1][:, PAIR:]) + total_ref[slot] * fade
        out_ref[slot] = (mix / total).astype(jnp.bfloat16)


def out_kernel(tokens, pos_ref, x_ref, weight, keep_ref, near_ref, far_ref):
    x = x_ref[...].reshape(2 * PADDED, 384)
    z = pos_ref[4]
    core = pos_ref[5]
    way = pos_ref[6]
    for refs, at_core, along in (((near_ref, far_ref), 1 - core, -way), ((keep_ref,), core, way)):
        for hop in range(SIDE):
            owner = wrap(z, hop * along) * 2 + at_core
            rows = weight[pl.ds(pl.multiple_of(owner * 384, 384), 384), :]
            part = lax.dot_general(
                x, rows, (((1,), (1,)), ((), ())), preferred_element_type=jnp.float32
            ).astype(jnp.bfloat16)
            for slot in range(2):
                ref, at = (refs[0], hop) if len(refs) == 1 else (refs[hop // 2], hop % 2)
                ref[2 * at + slot] = part[slot * PADDED : slot * PADDED + tokens]


SMEM = pl.BlockSpec(memory_space=pltpu.SMEM)
VMEM = pl.BlockSpec(memory_space=pltpu.VMEM)
ANY = pl.BlockSpec(memory_space=pl.ANY)


def call(kernel, out_shape, in_specs, scratch, name, flops, moved, vmem=48):
    out_specs = [VMEM] * len(out_shape) if isinstance(out_shape, list) else VMEM
    return pl.pallas_call(
        kernel,
        out_shape=out_shape,
        in_specs=in_specs,
        out_specs=out_specs,
        scratch_shapes=scratch,
        name=name,
        compiler_params=pltpu.CompilerParams(vmem_limit_bytes=vmem << 20),
        cost_estimate=pl.CostEstimate(flops=flops, bytes_accessed=moved, transcendentals=0),
    )


def struct(shape, dtype=jnp.bfloat16):
    return jax.ShapeDtypeStruct(shape, dtype)


def per_device(
    hidden_states,
    timestep_index,
    window_offsets,
    mod_weight,
    qkv_weight,
    query_gain,
    key_gain,
    out_weight,
    fresh_frame,
):
    tokens = hidden_states.shape[1]
    width = hidden_states.shape[2]
    place = lax.axis_index("frame")
    row = lax.axis_index("row")
    slots = 2 * lax.axis_size("frame")
    first_slot = 2 * place + 1
    x, y, z, core = place // SIDE, place % SIDE, row // 2, row % 2
    pos = jnp.where(core == 0, jnp.stack([y, x, 1, SIDE]), jnp.stack([x, y, SIDE, 1]))
    pos = jnp.concatenate([pos, jnp.stack([z, core, 1 - 2 * core, x, y, place])]).astype(jnp.int32)

    shard = jnp.concatenate(
        [qkv_weight[:, 1], qkv_weight[:, 2], qkv_weight[:, 0], out_weight.T], axis=0
    )

    plan = jnp.concatenate([timestep_index[:, None], window_offsets], axis=1)
    below = first_step(shard, 1)
    above = first_step(shard, -1)
    plan = spread(plan, "frame").reshape(slots, 3)
    shard, plan = together(shard, plan)
    own_b = second_step(shard, 1)
    own_a = second_step(shard, -1)
    waves = level_waves(jnp.roll(plan[:, 0], -1), place)
    sums = jnp.dot(waves, mod_weight.reshape(-1, 3 * width), preferred_element_type=jnp.float32)
    sums, first = together(sums, hidden_states[0])
    head = next_frame(first, -1)
    states = jnp.stack([hidden_states[1], head])
    sums = lax.all_to_all(sums.reshape(slots // 2, 2, 3 * width), "frame", 0, 0, tiled=True)
    travelling = jnp.pad(states, ((0, 0), (0, PADDED - tokens), (0, 0)))
    below, above, travelling, sums = together(below, above, travelling, sums)
    mods = jnp.sum(sums, axis=0)
    near_mods = lax.reduce_precision(mods, 8, 7)
    pieces = [near_mods[:, :width], (mods - near_mods)[:, :width]]
    pieces += [near_mods[:, width : 2 * width], (mods - near_mods)[:, width : 2 * width]]
    pieces = jnp.stack(pieces, axis=1).astype(jnp.bfloat16)
    travelling = lax.dynamic_update_slice(travelling, pieces, (0, tokens, 0))
    far = first_step(below, 1)
    below_b = second_step(below, 1)
    below_a = second_step(below, -1)
    above_b = second_step(above, 1)
    above_a = second_step(above, -1)
    z_b = z_step(travelling, 1)
    z_a = z_step(travelling, -1)
    far, z_b, z_a = together(far, z_b, z_a)
    far_b = second_step(far, 1)
    far_a = second_step(far, -1)
    own_f = second_step(own_b, 1)
    z_f = z_step(z_b, 1)
    below_f = second_step(below_b, 1)
    above_f = second_step(above_a, -1)
    far_f = second_step(far_a, -1)
    own_states = [travelling, z_b, z_a, z_f]
    other_states = [other_core(part) for part in own_states]
    shards = [
        shard, below, above, far,
        own_b, below_b, above_b, far_b,
        own_a, below_a, above_a, far_a,
        own_f, below_f, above_f, far_f,
    ]
    keys, values, modulated = pl.pallas_call(
        lambda *refs: key_value_kernel(tokens, *refs),
        out_shape=[struct((2, PADDED, width))] * 2 + [struct((2, PADDED, D))],
        in_specs=[SMEM, VMEM] + [ANY] * (8 + len(shards)),
        out_specs=[VMEM, VMEM, ANY],
        scratch_shapes=[
            pltpu.VMEM((8, 2, PADDED, width), jnp.bfloat16),
            pltpu.VMEM((2, PADDED, D), jnp.bfloat16),
            pltpu.VMEM((D, 2 * width), jnp.bfloat16),
            pltpu.SemaphoreType.DMA((2, 8)),
            pltpu.SemaphoreType.DMA,
            pltpu.SemaphoreType.DMA((2, 16)),
        ],
        name="keys_values",
        compiler_params=pltpu.CompilerParams(vmem_limit_bytes=60 << 20),
        cost_estimate=pl.CostEstimate(
            flops=4 * PADDED * D * 2 * width, bytes_accessed=D * width * 4 + PADDED * D * 4, transcendentals=0
        ),
    )(pos, key_gain[None], *own_states, *other_states, *shards)
    queries, out_whole = call(
        query_kernel,
        [struct((2, PADDED, width)), struct((D, width))],
        [SMEM, VMEM, VMEM] + [ANY] * len(shards),
        [pltpu.VMEM((D, width), jnp.bfloat16), pltpu.SemaphoreType.DMA((2, 16))],
        "queries",
        4 * PADDED * D * width,
        D * width * 4 + PADDED * D * 4,
        vmem=60,
    )(pos, modulated, query_gain[None], *shards)

    near = [next_frame(part, by) for part in (keys, values) for by in (1, -1)]
    far_kv = [next_frame(part, by) for part, by in zip(near, (1, -1, 1, -1))]

    block = pl.BlockSpec((2, PADDED, PAIR), lambda pair: (0, 0, pair))
    params = pltpu.CompilerParams(vmem_limit_bytes=48 << 20)
    mix, total, top = pl.pallas_call(
        lambda *refs: near_kernel(tokens, *refs),
        out_shape=[struct((2, PADDED, width), jnp.float32)] * 3,
        grid=(3,),
        in_specs=[SMEM, SMEM] + [block] * 7,
        out_specs=[block] * 3,
        scratch_shapes=[
            pltpu.VMEM((6, KEYS, PAIR), jnp.bfloat16),
            pltpu.VMEM((6, KEYS, 2 * PAIR), jnp.bfloat16),
        ],
        name="attention_near",
        compiler_params=params,
        cost_estimate=pl.CostEstimate(
            flops=6 * 6 * 4 * 480 * 256 * 256, bytes_accessed=6 << 20, transcendentals=36 * 480 * 256
        ),
    )(plan, pos, queries, near[0], near[2], keys, values, near[1], near[3])
    mixed = pl.pallas_call(
        lambda *refs: far_kernel(tokens, *refs),
        out_shape=struct((2, PADDED, width)),
        grid=(3,),
        in_specs=[SMEM, SMEM] + [block] * 8,
        out_specs=block,
        scratch_shapes=[
            pltpu.VMEM((4, KEYS, PAIR), jnp.bfloat16),
            pltpu.VMEM((4, KEYS, 2 * PAIR), jnp.bfloat16),
        ],
        name="attention_far",
        compiler_params=params,
        cost_estimate=pl.CostEstimate(
            flops=6 * 3 * 4 * 480 * 256 * 256, bytes_accessed=6 << 20, transcendentals=18 * 480 * 256
        ),
    )(plan, pos, queries, far_kv[0], far_kv[2], far_kv[1], far_kv[3], mix, total, top)
    keep, send_near, send_far = call(
        lambda *refs: out_kernel(tokens, *refs),
        [struct((2 * SIDE, tokens, width))] + [struct((SIDE, tokens, width))] * 2,
        [SMEM, VMEM, VMEM],
        [],
        "out_projection",
        4 * PADDED * D * width,
        D * width * 2 + PADDED * D * 4,
    )(pos, mixed, out_whole)

    swapped_far = other_core(send_far)
    swapped_near = other_core(send_near)

    def on_chip(hop):
        swapped = (swapped_near, swapped_far)[hop // 2][hop % 2 * 2 : hop % 2 * 2 + 2]
        return keep[2 * hop : 2 * hop + 2].astype(jnp.float32) + swapped.astype(jnp.float32)

    onward = z_step(on_chip(2).astype(jnp.bfloat16), 1)
    back = z_step(on_chip(3).astype(jnp.bfloat16), -1)
    forth = z_step((on_chip(1) + onward.astype(jnp.float32)).astype(jnp.bfloat16), 1)
    attended = on_chip(0) + back.astype(jnp.float32) + forth.astype(jnp.float32)
    gate = mods[:, None, 2 * width :]
    updated = (states.astype(jnp.float32) + gate * attended).astype(jnp.bfloat16)
    spare = (first_slot + jnp.arange(2) == slots)[:, None, None]
    return jnp.where(spare, fresh_frame[None], updated)


def solution(mesh):
    return jax.shard_map(
        per_device,
        mesh=mesh,
        in_specs=(
            P("frame", None, "row"),
            P("frame"),
            P("frame", None),
            P("frame", None, "row"),
            P("frame", None, "row"),
            P(),
            P(),
            P("row", "frame"),
            P(None, "row"),
        ),
        out_specs=P("frame", None, "row"),
        check_vma=False,
    )
```

```python
import math

import jax
import jax.numpy as jnp
from jax import lax
from jax.experimental import pallas as pl
from jax.experimental.pallas import tpu as pltpu
from jax.sharding import PartitionSpec as P

HEAD = 64
D = 3072
TEMB = 512
REACH = 4
SIDE = 4
PADDED = 240
KEYS = 256
PAIR = 2 * HEAD
ORIGIN = (0, -1, 1, 2)


def torus_step(array, move):
    pairs = []
    for x in range(SIDE):
        for y in range(SIDE):
            for z in range(SIDE):
                for core in range(2):
                    to_x, to_y, to_z = (part % SIDE for part in move(x, y, z, core))
                    pairs.append((device_at(x, y, z, core), device_at(to_x, to_y, to_z, core)))
    return lax.ppermute(array, ("frame", "row"), pairs)


def device_at(x, y, z, core):
    return (x * SIDE + y) * 2 * SIDE + z * 2 + core


def first_step(array, by):
    return torus_step(array, lambda x, y, z, core: (x + by * core, y + by * (1 - core), z))


def second_step(array, by):
    return torus_step(array, lambda x, y, z, core: (x + by * (1 - core), y + by * core, z))


def z_step(array, by):
    return torus_step(array, lambda x, y, z, core: (x, y, z + by * (1 - 2 * core)))


def other_core(array):
    pairs = [(z * 2 + c, z * 2 + 1 - c) for z in range(SIDE) for c in range(2)]
    return lax.ppermute(array, "row", pairs)


def next_frame(array, by):
    peers = lax.axis_size("frame")
    return lax.ppermute(array, "frame", [(i, (i + by) % peers) for i in range(peers)])


def together(*values):
    return lax.optimization_barrier(values)


def level_waves(levels, place):
    half = TEMB // 2
    rows = TEMB // lax.axis_size("frame")
    entry = place * rows + jnp.arange(rows)
    freqs = jnp.exp(-math.log(10000.0) * (entry % half).astype(jnp.float32) / half)
    angles = levels.astype(jnp.float32)[:, None] * freqs[None, :]
    waves = jnp.where(entry[None, :] < half, jnp.cos(angles), jnp.sin(angles))
    return jax.nn.silu(waves).astype(jnp.bfloat16)


def spread(array, axis):
    copies = jnp.broadcast_to(array[None], (lax.axis_size(axis),) + array.shape)
    return lax.all_to_all(copies, axis, 0, 0, tiled=True)


def wrap(value, by):
    return lax.rem(value + by + SIDE, SIDE)


def shard_copies(places, pos_ref, target, column, sems):
    copies = []
    for outer in range(SIDE):
        for inner in range(SIDE):
            owner = wrap(pos_ref[1], ORIGIN[outer]) * pos_ref[3] + wrap(pos_ref[0], ORIGIN[inner]) * pos_ref[2]
            rows = pl.ds(pl.multiple_of(owner * 192, 192), 192)
            copies.append(
                pltpu.make_async_copy(
                    places[outer][inner], target.at[rows, column : column + 384], sems.at[len(copies)]
                )
            )
    return copies


def head_norm_pair(values, gain_ref):
    low = lax.broadcasted_iota(jnp.int32, values.shape, 1) < HEAD

    def mean_of(array):
        first = jnp.sum(jnp.where(low, array, 0.0), axis=1, keepdims=True)
        second = jnp.sum(jnp.where(low, 0.0, array), axis=1, keepdims=True)
        return jnp.where(low, first, second) * (1.0 / HEAD)

    gain = jnp.concatenate([gain_ref[...], gain_ref[...]], axis=1)
    centered = values - mean_of(values)
    spread = mean_of(centered * centered)
    return (centered * lax.rsqrt(spread + 1e-06) * gain).astype(jnp.bfloat16)


def modulate(tokens, pos_ref, own_refs, other_refs, out_ref, arriving):
    width = own_refs[0].shape[2]
    z = pos_ref[4]
    core = pos_ref[5]
    way = pos_ref[6]
    for slot in range(2):
        for copy in arriving[slot]:
            copy.wait()
        total = jnp.zeros((tokens, width), jnp.float32)
        square = jnp.zeros((tokens, width), jnp.float32)
        for ref in (*own_refs, *other_refs):
            part = ref[slot, 0:tokens, :].astype(jnp.float32)
            total += part
            square += part * part
        mean = jnp.sum(total, axis=1, keepdims=True) * (1.0 / D)
        meansq = jnp.sum(square, axis=1, keepdims=True) * (1.0 / D)
        inverse = lax.rsqrt(meansq - mean * mean + 1e-05)
        for refs_of, at_core, along in ((own_refs, core, way), (other_refs, 1 - core, -way)):
            for hop in range(SIDE):
                part = refs_of[hop][slot, 0:tokens, :].astype(jnp.float32)
                last = refs_of[hop][slot, tokens // 16 * 16 : PADDED, :].astype(jnp.float32)
                first = tokens % 16
                normed = (part - mean) * inverse
                owner = wrap(z, ORIGIN[hop] * along) * 2 + at_core
                shift = last[first : first + 1] + last[first + 1 : first + 2]
                scale = last[first + 2 : first + 3] + last[first + 3 : first + 4]
                columns = pl.ds(pl.multiple_of(owner * width, width), width)
                out_ref[slot, 0:tokens, columns] = (normed * (1.0 + scale) + shift).astype(jnp.bfloat16)
        out_ref[slot, tokens:, :] = jnp.zeros((PADDED - tokens, D), jnp.bfloat16)


def shard_places(shards, top):
    return [[shards[SIDE * outer + inner].at[pl.ds(top, 192)] for inner in range(SIDE)] for outer in range(SIDE)]


def key_value_kernel(tokens, pos_ref, gain_ref, *refs):
    given, shards = refs[:8], refs[8:24]
    k_ref, v_ref, x_ref, held, modulated, weight, held_sems, x_sem, sems = refs[24:]
    states = [held.at[part] for part in range(8)]
    arriving = [
        [
            pltpu.make_async_copy(given[part].at[slot], states[part].at[slot], held_sems.at[slot, part])
            for part in range(8)
        ]
        for slot in range(2)
    ]
    for copy in sum(arriving, []):
        copy.start()
    copies = [
        shard_copies(shard_places(shards, part * 192), pos_ref, weight, part * 384, sems.at[part])
        for part in range(2)
    ]
    for copy in sum(copies, []):
        copy.start()
    modulate(tokens, pos_ref, states[:SIDE], states[SIDE:], modulated, arriving)
    x_copy = pltpu.make_async_copy(modulated, x_ref, x_sem)
    x_copy.start()
    x = modulated[...].reshape(2 * PADDED, D)
    for group in range(6):
        if group in (0, 2):
            for copy in copies[group // 2]:
                copy.wait()
        if group % 2 == 0:
            both = jnp.dot(
                x, weight[:, group * PAIR : (group + 2) * PAIR], preferred_element_type=jnp.float32
            )
        piece = both[:, group % 2 * PAIR : (group % 2 + 1) * PAIR]
        columns = slice(group % 3 * PAIR, (group % 3 + 1) * PAIR)
        piece = head_norm_pair(piece, gain_ref) if group < 3 else piece.astype(jnp.bfloat16)
        for slot in range(2):
            (k_ref, v_ref)[group // 3][slot, :, columns] = piece[slot * PADDED : (slot + 1) * PADDED]
    x_copy.wait()


def query_kernel(pos_ref, x_ref, gain_ref, *refs):
    shards, (q_ref, out_weight_ref, weight, sems) = refs[:16], refs[16:]
    copies = shard_copies(shard_places(shards, 384), pos_ref, weight, 0, sems.at[0])
    copies += shard_copies(shard_places(shards, 576), pos_ref, out_weight_ref, 0, sems.at[1])
    for copy in copies:
        copy.start()
    for copy in copies:
        copy.wait()
    x = x_ref[...].reshape(2 * PADDED, D)
    whole = jnp.dot(x, weight[...], preferred_element_type=jnp.float32)
    for pair in range(3):
        columns = slice(pair * PAIR, (pair + 1) * PAIR)
        piece = head_norm_pair(whole[:, columns], gain_ref) * jnp.asarray(1.0 / math.sqrt(HEAD), jnp.bfloat16)
        for slot in range(2):
            q_ref[slot, :, columns] = piece[slot * PADDED : (slot + 1) * PADDED]


def fill_window(pairs, keys, values):
    for index, (key_ref, value_ref) in enumerate(pairs):
        for half in range(2):
            slot = 2 * index + half
            keys[slot, 0:PADDED, :] = key_ref[half]
            keys[slot, PADDED:, :] = jnp.zeros((KEYS - PADDED, PAIR), jnp.bfloat16)
            values[slot, 0:PADDED, 0:PAIR] = value_ref[half]
            values[slot, PADDED:, 0:PAIR] = jnp.zeros((KEYS - PADDED, PAIR), jnp.bfloat16)
            values[slot, :, PAIR:] = jnp.ones((KEYS, PAIR), jnp.bfloat16)


def seen_bias(plan_ref, pos_ref, slot, window, tokens):
    first = 2 * pos_ref[9] + 1
    at = lax.rem(first + slot, plan_ref.shape[0])
    lowest = jnp.maximum(slot - plan_ref[at, 1], -first)
    highest = jnp.minimum(slot + plan_ref[at, 2], plan_ref.shape[0] - 1 - first)
    column = lax.broadcasted_iota(jnp.int32, (1, KEYS), 1)
    parts = []
    for relative in window:
        known = jnp.logical_and(relative >= lowest, relative <= highest)
        count = jnp.where(known, tokens, 0)
        parts.append(jnp.where(column < count, 0.0, -jnp.inf))
    return jnp.concatenate(parts, axis=1)


def near_kernel(tokens, plan_ref, pos_ref, q_ref, km, vm, ko, vo, kp, vp, mix_ref, total_ref, top_ref, keys, values):
    fill_window(((km, vm), (ko, vo), (kp, vp)), keys, values)
    low = lax.broadcasted_iota(jnp.int32, (PADDED, PAIR), 1) < HEAD
    key_win = keys[...].reshape(6 * KEYS, PAIR)
    value_win = values[...].reshape(6 * KEYS, 2 * PAIR)
    for slot in range(2):
        query = q_ref[slot]
        bias = seen_bias(plan_ref, pos_ref, slot, range(-2, 4), tokens)
        nothing = jnp.zeros_like(query)
        mixes = []
        peaks = []
        for one in (jnp.where(low, query, nothing), jnp.where(low, nothing, query)):
            scores = lax.dot_general(
                one, key_win, (((1,), (1,)), ((), ())), preferred_element_type=jnp.float32
            )
            scores = scores + bias
            peak = jnp.max(scores, axis=1, keepdims=True)
            expo = jnp.exp(scores - peak).astype(jnp.bfloat16)
            mixes.append(jnp.dot(expo, value_win, preferred_element_type=jnp.float32))
            peaks.append(jnp.broadcast_to(peak, (PADDED, PAIR)))
        mix_ref[slot] = jnp.where(low, mixes[0][:, :PAIR], mixes[1][:, :PAIR])
        total_ref[slot] = jnp.where(low, mixes[0][:, PAIR:], mixes[1][:, PAIR:])
        top_ref[slot] = jnp.where(low, peaks[0], peaks[1])


def far_kernel(tokens, plan_ref, pos_ref, q_ref, km, vm, kp, vp, mix_ref, total_ref, top_ref, out_ref, keys, values):
    fill_window(((km, vm), (kp, vp)), keys, values)
    low = lax.broadcasted_iota(jnp.int32, (PADDED, PAIR), 1) < HEAD
    window = (-4, -3, 4, 5)
    for slot in range(2):
        query = q_ref[slot]
        bias = seen_bias(plan_ref, pos_ref, slot, window[slot : slot + 3], tokens)
        nothing = jnp.zeros_like(query)
        key_win = keys[slot : slot + 3].reshape(3 * KEYS, PAIR)
        value_win = values[slot : slot + 3].reshape(3 * KEYS, 2 * PAIR)
        near_top = top_ref[slot]
        mixes = []
        peaks = []
        for head, one in enumerate((jnp.where(low, query, nothing), jnp.where(low, nothing, query))):
            scores = lax.dot_general(
                one, key_win, (((1,), (1,)), ((), ())), preferred_element_type=jnp.float32
            )
            scores = scores + bias
            peak = jnp.maximum(
                jnp.max(scores, axis=1, keepdims=True), near_top[:, head * HEAD : head * HEAD + 1]
            )
            expo = jnp.exp(scores - peak).astype(jnp.bfloat16)
            mixes.append(jnp.dot(expo, value_win, preferred_element_type=jnp.float32))
            peaks.append(jnp.broadcast_to(peak, (PADDED, PAIR)))
        fade = jnp.exp(near_top - jnp.where(low, peaks[0], peaks[1]))
        mix = jnp.where(low, mixes[0][:, :PAIR], mixes[1][:, :PAIR]) + mix_ref[slot] * fade
        total = jnp.where(low, mixes[0][:, PAIR:], mixes[1][:, PAIR:]) + total_ref[slot] * fade
        out_ref[slot] = (mix / total).astype(jnp.bfloat16)


def out_kernel(tokens, pos_ref, x_ref, weight, keep_ref, near_ref, far_ref):
    x = x_ref[...].reshape(2 * PADDED, 384)
    z = pos_ref[4]
    core = pos_ref[5]
    way = pos_ref[6]
    for refs, at_core, along in (((near_ref, far_ref), 1 - core, -way), ((keep_ref,), core, way)):
        for hop in range(SIDE):
            owner = wrap(z, hop * along) * 2 + at_core
            rows = weight[pl.ds(pl.multiple_of(owner * 384, 384), 384), :]
            part = lax.dot_general(
                x, rows, (((1,), (1,)), ((), ())), preferred_element_type=jnp.float32
            ).astype(jnp.bfloat16)
            for slot in range(2):
                ref, at = (refs[0], hop) if len(refs) == 1 else (refs[hop // 2], hop % 2)
                ref[2 * at + slot] = part[slot * PADDED : slot * PADDED + tokens]


SMEM = pl.BlockSpec(memory_space=pltpu.SMEM)
VMEM = pl.BlockSpec(memory_space=pltpu.VMEM)
ANY = pl.BlockSpec(memory_space=pl.ANY)


def call(kernel, out_shape, in_specs, scratch, name, flops, moved, vmem=48):
    out_specs = [VMEM] * len(out_shape) if isinstance(out_shape, list) else VMEM
    return pl.pallas_call(
        kernel,
        out_shape=out_shape,
        in_specs=in_specs,
        out_specs=out_specs,
        scratch_shapes=scratch,
        name=name,
        compiler_params=pltpu.CompilerParams(vmem_limit_bytes=vmem << 20),
        cost_estimate=pl.CostEstimate(flops=flops, bytes_accessed=moved, transcendentals=0),
    )


def struct(shape, dtype=jnp.bfloat16):
    return jax.ShapeDtypeStruct(shape, dtype)


def per_device(
    hidden_states,
    timestep_index,
    window_offsets,
    mod_weight,
    qkv_weight,
    query_gain,
    key_gain,
    out_weight,
    fresh_frame,
):
    tokens = hidden_states.shape[1]
    width = hidden_states.shape[2]
    place = lax.axis_index("frame")
    row = lax.axis_index("row")
    slots = 2 * lax.axis_size("frame")
    first_slot = 2 * place + 1
    x, y, z, core = place // SIDE, place % SIDE, row // 2, row % 2
    pos = jnp.where(core == 0, jnp.stack([y, x, 1, SIDE]), jnp.stack([x, y, SIDE, 1]))
    pos = jnp.concatenate([pos, jnp.stack([z, core, 1 - 2 * core, x, y, place])]).astype(jnp.int32)

    shard = jnp.concatenate(
        [qkv_weight[:, 1], qkv_weight[:, 2], qkv_weight[:, 0], out_weight.T], axis=0
    )

    plan = jnp.concatenate([timestep_index[:, None], window_offsets], axis=1)
    below = first_step(shard, 1)
    above = first_step(shard, -1)
    plan = spread(plan, "frame").reshape(slots, 3)
    shard, plan = together(shard, plan)
    own_b = second_step(shard, 1)
    own_a = second_step(shard, -1)
    waves = level_waves(jnp.roll(plan[:, 0], -1), place)
    sums = jnp.dot(waves, mod_weight.reshape(-1, 3 * width), preferred_element_type=jnp.float32)
    sums, first = together(sums, hidden_states[0])
    head = next_frame(first, -1)
    states = jnp.stack([hidden_states[1], head])
    sums = lax.all_to_all(sums.reshape(slots // 2, 2, 3 * width), "frame", 0, 0, tiled=True)
    travelling = jnp.pad(states, ((0, 0), (0, PADDED - tokens), (0, 0)))
    below, above, travelling, sums = together(below, above, travelling, sums)
    mods = jnp.sum(sums, axis=0)
    near_mods = lax.reduce_precision(mods, 8, 7)
    pieces = [near_mods[:, :width], (mods - near_mods)[:, :width]]
    pieces += [near_mods[:, width : 2 * width], (mods - near_mods)[:, width : 2 * width]]
    pieces = jnp.stack(pieces, axis=1).astype(jnp.bfloat16)
    travelling = lax.dynamic_update_slice(travelling, pieces, (0, tokens, 0))
    far = first_step(below, 1)
    below_b = second_step(below, 1)
    below_a = second_step(below, -1)
    above_b = second_step(above, 1)
    above_a = second_step(above, -1)
    z_b = z_step(travelling, 1)
    z_a = z_step(travelling, -1)
    far, z_b, z_a = together(far, z_b, z_a)
    far_b = second_step(far, 1)
    far_a = second_step(far, -1)
    own_f = second_step(own_b, 1)
    z_f = z_step(z_b, 1)
    below_f = second_step(below_b, 1)
    above_f = second_step(above_a, -1)
    far_f = second_step(far_a, -1)
    own_states = [travelling, z_b, z_a, z_f]
    other_states = [other_core(part) for part in own_states]
    shards = [
        shard, below, above, far,
        own_b, below_b, above_b, far_b,
        own_a, below_a, above_a, far_a,
        own_f, below_f, above_f, far_f,
    ]
    keys, values, modulated = pl.pallas_call(
        lambda *refs: key_value_kernel(tokens, *refs),
        out_shape=[struct((2, PADDED, width))] * 2 + [struct((2, PADDED, D))],
        in_specs=[SMEM, VMEM] + [ANY] * (8 + len(shards)),
        out_specs=[VMEM, VMEM, ANY],
        scratch_shapes=[
            pltpu.VMEM((8, 2, PADDED, width), jnp.bfloat16),
            pltpu.VMEM((2, PADDED, D), jnp.bfloat16),
            pltpu.VMEM((D, 2 * width), jnp.bfloat16),
            pltpu.SemaphoreType.DMA((2, 8)),
            pltpu.SemaphoreType.DMA,
            pltpu.SemaphoreType.DMA((2, 16)),
        ],
        name="keys_values",
        compiler_params=pltpu.CompilerParams(vmem_limit_bytes=60 << 20),
        cost_estimate=pl.CostEstimate(
            flops=4 * PADDED * D * 2 * width, bytes_accessed=D * width * 4 + PADDED * D * 4, transcendentals=0
        ),
    )(pos, key_gain[None], *own_states, *other_states, *shards)
    queries, out_whole = call(
        query_kernel,
        [struct((2, PADDED, width)), struct((D, width))],
        [SMEM, VMEM, VMEM] + [ANY] * len(shards),
        [pltpu.VMEM((D, width), jnp.bfloat16), pltpu.SemaphoreType.DMA((2, 16))],
        "queries",
        4 * PADDED * D * width,
        D * width * 4 + PADDED * D * 4,
        vmem=60,
    )(pos, modulated, query_gain[None], *shards)

    near = [next_frame(part, by) for part in (keys, values) for by in (1, -1)]
    far_kv = [next_frame(part, by) for part, by in zip(near, (1, -1, 1, -1))]

    block = pl.BlockSpec((2, PADDED, PAIR), lambda pair: (0, 0, pair))
    params = pltpu.CompilerParams(vmem_limit_bytes=48 << 20)
    mix, total, top = pl.pallas_call(
        lambda *refs: near_kernel(tokens, *refs),
        out_shape=[struct((2, PADDED, width), jnp.float32)] * 3,
        grid=(3,),
        in_specs=[SMEM, SMEM] + [block] * 7,
        out_specs=[block] * 3,
        scratch_shapes=[
            pltpu.VMEM((6, KEYS, PAIR), jnp.bfloat16),
            pltpu.VMEM((6, KEYS, 2 * PAIR), jnp.bfloat16),
        ],
        name="attention_near",
        compiler_params=pltpu.CompilerParams(vmem_limit_bytes=60 << 20),
        cost_estimate=pl.CostEstimate(
            flops=6 * 6 * 4 * 480 * 256 * 256, bytes_accessed=6 << 20, transcendentals=36 * 480 * 256
        ),
    )(plan, pos, queries, near[0], near[2], keys, values, near[1], near[3])
    mixed = pl.pallas_call(
        lambda *refs: far_kernel(tokens, *refs),
        out_shape=struct((2, PADDED, width)),
        grid=(3,),
        in_specs=[SMEM, SMEM] + [block] * 8,
        out_specs=block,
        scratch_shapes=[
            pltpu.VMEM((4, KEYS, PAIR), jnp.bfloat16),
            pltpu.VMEM((4, KEYS, 2 * PAIR), jnp.bfloat16),
        ],
        name="attention_far",
        compiler_params=params,
        cost_estimate=pl.CostEstimate(
            flops=6 * 3 * 4 * 480 * 256 * 256, bytes_accessed=6 << 20, transcendentals=18 * 480 * 256
        ),
    )(plan, pos, queries, far_kv[0], far_kv[2], far_kv[1], far_kv[3], mix, total, top)
    keep, send_near, send_far = call(
        lambda *refs: out_kernel(tokens, *refs),
        [struct((2 * SIDE, tokens, width))] + [struct((SIDE, tokens, width))] * 2,
        [SMEM, VMEM, VMEM],
        [],
        "out_projection",
        4 * PADDED * D * width,
        D * width * 2 + PADDED * D * 4,
    )(pos, mixed, out_whole)

    swapped_far = other_core(send_far)
    swapped_near = other_core(send_near)

    def on_chip(hop):
        swapped = (swapped_near, swapped_far)[hop // 2][hop % 2 * 2 : hop % 2 * 2 + 2]
        return keep[2 * hop : 2 * hop + 2].astype(jnp.float32) + swapped.astype(jnp.float32)

    onward = z_step(on_chip(2).astype(jnp.bfloat16), 1)
    back = z_step(on_chip(3).astype(jnp.bfloat16), -1)
    forth = z_step((on_chip(1) + onward.astype(jnp.float32)).astype(jnp.bfloat16), 1)
    attended = on_chip(0) + back.astype(jnp.float32) + forth.astype(jnp.float32)
    gate = mods[:, None, 2 * width :]
    updated = (states.astype(jnp.float32) + gate * attended).astype(jnp.bfloat16)
    spare = (first_slot + jnp.arange(2) == slots)[:, None, None]
    return jnp.where(spare, fresh_frame[None], updated)


def solution(mesh):
    return jax.shard_map(
        per_device,
        mesh=mesh,
        in_specs=(
            P("frame", None, "row"),
            P("frame"),
            P("frame", None),
            P("frame", None, "row"),
            P("frame", None, "row"),
            P(),
            P(),
            P("row", "frame"),
            P(None, "row"),
        ),
        out_specs=P("frame", None, "row"),
        check_vma=False,
    )
```
